512 devices in a mesh: dp: 64 (over z, x), expert: 8 (over y, core).
Axes of the slice: x: 4, y: 4, z: 16, core: 2. Of those that a mesh axis runs over, the one named last changes fastest.
Arguments:
- gradient: float32 [64, 768, 1024], P('expert', 'dp'), may hold values from -400 to 400
- momentum: float32 [64, 768, 1024], P('expert', 'dp'), may hold values from -100 to 100
Outputs:
- momentum_next: float32 [64, 768, 1024], P('expert', 'dp')
- update: bfloat16 [64, 768, 1024], P('expert', 'dp')
The draws below stay inside these ranges and needn't reach their ends.
All inputs are finite; a program needn't handle non-finite values.
Results may differ from the reference program's by a relative error of at most 0.0063.
Values may be sent and summed in bfloat16 or wider, within the bound.
No kernel may reach another device: no remote copies, remote signals or barrier semaphores. Data moves between devices by JAX's collectives and lax.ppermute only.
A program may use at most 64 MiB of HBM per device.

```python
import math
import jax
import jax.numpy as jnp
from jax import lax

D = 1024
FF = 768
MATS = 8
ITERS = 2
GROUPS_MATS = 64


def field_scales(key):
    first_key, second_key, group_key = jax.random.split(key, 3)
    row_scale = jnp.exp(jax.random.uniform(first_key, (GROUPS_MATS, FF, 1), jnp.float32) * math.log(10.0))
    rising = (1.0 + 2.0 * jnp.arange(FF, dtype=jnp.float32) / (FF - 1))[None, :, None]
    column_scale = jnp.exp(jax.random.uniform(second_key, (GROUPS_MATS, 1, D), jnp.float32) * math.log(10.0))
    groups = GROUPS_MATS // MATS
    group_index = (jnp.arange(GROUPS_MATS) // MATS).astype(jnp.float32)
    rising_groups = 0.6 + 0.4 * group_index / max(groups - 1, 1)
    chosen = jax.random.randint(group_key, (), 0, groups).astype(jnp.float32)
    group_scale = rising_groups * jnp.where(group_index == chosen, 3.5, 1.0) / 3.5
    return row_scale * rising * column_scale * group_scale[:, None, None]


def draw_gradient(key, part):
    key = jax.random.fold_in(key, 11)
    base_key, scale_key = jax.random.split(key, 2)
    scales = field_scales(scale_key)
    base = jax.random.truncated_normal(base_key, -6.0, 6.0, (GROUPS_MATS, FF, D), jnp.float32)
    return 0.1 * base * scales


def draw_momentum(key, part):
    key = jax.random.fold_in(key, 23)
    base_key, scale_key = jax.random.split(key, 2)
    scales = field_scales(scale_key)
    base = jax.random.truncated_normal(base_key, -6.0, 6.0, (GROUPS_MATS, FF, D), jnp.float32)
    return 0.024 * base * scales


def setup_inputs(seed: int = 0) -> dict:
    splits = jax.random.split(jax.random.key(seed), 3)
    return {
        "gradient": draw_gradient(jax.random.fold_in(splits[2], 71), 0),
        "momentum": draw_momentum(jax.random.fold_in(splits[2], 71), 0),
    }


MOMENTUM_RATE = 0.95
RMS_CAP = 0.5
NORM_EPS = 1e-07
COEF_A = 3.4445
COEF_B = -4.775
COEF_C = 2.0315

def orthogonalize(initial):
    iterate = initial
    combined = initial.astype(jnp.float32)
    for number in range(ITERS):
        gram_matrix = jnp.dot(iterate, iterate.T, preferred_element_type=jnp.float32).astype(jnp.bfloat16)
        squared = jnp.dot(gram_matrix, gram_matrix, preferred_element_type=jnp.float32)
        polynomial = (COEF_B * gram_matrix.astype(jnp.float32) + COEF_C * squared).astype(jnp.bfloat16)
        combined = COEF_A * iterate.astype(jnp.float32) + jnp.dot(polynomial, iterate, preferred_element_type=jnp.float32)
        if number + 1 < ITERS:
            iterate = combined.astype(jnp.bfloat16)
    return (0.2 * math.sqrt(max(FF, D)) * combined).astype(jnp.bfloat16)

def reference(gradient, momentum):
    total_square = jnp.sum(gradient * gradient)
    factor = jnp.minimum(1.0, RMS_CAP * math.sqrt(GROUPS_MATS * FF * D) / jnp.sqrt(total_square))
    momentum_next = MOMENTUM_RATE * momentum + factor * gradient
    blended = factor * gradient + MOMENTUM_RATE * momentum_next
    norm_square = lax.optimization_barrier(jnp.sum(blended * blended, axis=(1, 2)))
    initial = (blended / (jnp.sqrt(norm_square) + NORM_EPS)[:, None, None]).astype(jnp.bfloat16)
    update = lax.map(orthogonalize, initial)
    return (momentum_next, update)
```

```python
import math

import jax
import jax.numpy as jnp
from jax import lax
from jax.experimental import pallas as pl
from jax.experimental.pallas import tpu as pltpu
from jax.sharding import Mesh, PartitionSpec as P

D = 1024
FF = 768
MATS = 8
HALF = D // 2
TILE = 256
PLANES = ((0, 2, 4, 6, 9, 11, 13, 15), (1, 3, 5, 7, 8, 10, 12, 14))
SHIFTS = (2, 3, 1)


MOMENTUM_RATE = 0.95
RMS_CAP = 0.5
NORM_EPS = 1e-07
COEF_A = 3.4445
COEF_B = -4.775
COEF_C = 2.0315


def dot_f32(left, right):
    return jnp.dot(left, right, preferred_element_type=jnp.float32)


def dot_transposed(left, right):
    return lax.dot_general(left, right, (((1,), (1,)), ((), ())), preferred_element_type=jnp.float32)


def call(kernel, out_shape, *args, scratch=(), cost=None, space=pltpu.VMEM, limit=32768):
    return pl.pallas_call(
        kernel,
        out_shape=out_shape,
        in_specs=[pl.BlockSpec(memory_space=space)] * len(args),
        out_specs=jax.tree.map(lambda _: pl.BlockSpec(memory_space=pltpu.VMEM), out_shape),
        scratch_shapes=scratch,
        compiler_params=pltpu.CompilerParams(vmem_limit_bytes=limit * 1024),
        cost_estimate=cost,
    )(*args)


def start_kernel(gradient, momentum, sums, kept, decayed, arrivals):
    copies = [
        pltpu.make_async_copy(gradient, kept, arrivals.at[0]),
        pltpu.make_async_copy(momentum, decayed, arrivals.at[1]),
    ]
    for copy in copies:
        copy.start()
    copies[0].wait()
    value = kept[...]
    sums[...] = jnp.broadcast_to(jnp.sum(value * value), sums.shape)
    copies[1].wait()
    decayed[...] = MOMENTUM_RATE * decayed[...]


def add_kernel(parts, out):
    out[...] = jnp.broadcast_to(jnp.sum(parts[...], axis=0, keepdims=True), out.shape)


def blend_kernel(total, gradient, decayed, momentum_next, outgoing):
    total_square = jnp.sum(total[...], axis=0)[:, :1]
    factor = jnp.minimum(1.0, RMS_CAP * math.sqrt(MATS * MATS * FF * D) / jnp.sqrt(total_square))
    scaled = factor[None] * gradient[...]
    following = decayed[...] + scaled
    momentum_next[...] = following
    blended = jnp.swapaxes(scaled + MOMENTUM_RATE * following, 0, 1)
    left, right = blended[:, :, :HALF], blended[:, :, HALF:]
    packed = jnp.concatenate([left[:, :8], right[:, :8], left[:, 8:], right[:, 8:]], axis=1)
    outgoing[...] = packed.astype(jnp.bfloat16)


def unpacked(value):
    left, right = [], []
    for number in range(0, MATS, 2):
        first, second = value[number], value[number + 1]
        left += [first[:8], second[:8], first[16:20], second[16:20]]
        right += [first[8:16], second[8:16], first[20:], second[20:]]
    return jnp.concatenate(left, axis=0), jnp.concatenate(right, axis=0)


def packed_blocks(left, right):
    blocks = []
    for start in range(0, left.shape[0], 24):
        for place in range(2):
            head, tail = start + 8 * place, start + 16 + 4 * place
            blocks.append(
                jnp.concatenate(
                    [left[head : head + 8], right[head : head + 8], left[tail : tail + 4], right[tail : tail + 4]],
                    axis=0,
                )
            )
    return blocks


def orthogonal_kernel(*refs):
    pieces, (out, whole, product, gram, poly, second) = refs[:MATS], refs[MATS:]
    rows = FF // MATS
    tiles = [slice(start, start + TILE) for start in range(0, FF, TILE)]
    for number, piece in enumerate(pieces):
        left, right = unpacked(piece[...].astype(jnp.float32))
        place = slice(number * rows, (number + 1) * rows)
        whole[place, :HALF] = left.astype(jnp.bfloat16)
        whole[place, HALF:] = right.astype(jnp.bfloat16)
    on_diagonal = lax.broadcasted_iota(jnp.int32, (TILE, TILE), 0) == lax.broadcasted_iota(
        jnp.int32, (TILE, TILE), 1
    )
    norm_square = jnp.float32(0.0)
    for tile in tiles:
        product[tile, :] = dot_transposed(whole[tile, :], whole[...])
        norm_square += jnp.sum(jnp.where(on_diagonal, product[tile, tile], 0.0))
    inverse = 1.0 / (jnp.sqrt(jnp.full((1, 1), norm_square, jnp.float32)) + NORM_EPS)
    for tile in tiles:
        gram[tile, :] = (product[tile, :] * (inverse * inverse)).astype(jnp.bfloat16)
    for tile in tiles:
        squared = dot_f32(gram[tile, :], gram[...])
        poly[tile, :] = (COEF_B * gram[tile, :].astype(jnp.float32) + COEF_C * squared).astype(
            jnp.bfloat16
        )
    for tile in tiles:
        combined = COEF_A * whole[tile, :].astype(jnp.float32) + dot_f32(poly[tile, :], whole[...])
        second[tile, :] = (inverse * combined).astype(jnp.bfloat16)
    for tile in tiles:
        gram[tile, :] = dot_transposed(second[tile, :], second[...]).astype(jnp.bfloat16)
    own = gram[:rows, :]
    own_poly = (COEF_B * own.astype(jnp.float32) + COEF_C * dot_f32(own, gram[...])).astype(
        jnp.bfloat16
    )
    combined = COEF_A * second[:rows, :].astype(jnp.float32) + dot_f32(own_poly, second[...])
    scaled = 0.2 * math.sqrt(max(FF, D)) * combined
    for number, block in enumerate(packed_blocks(scaled[:, :HALF], scaled[:, HALF:])):
        out[number] = block.astype(jnp.bfloat16)


def spread_kernel(arrived, out):
    value = arrived[...].astype(jnp.float32)
    left = jnp.concatenate([value[:, :8], value[:, 16:20]], axis=1)
    right = jnp.concatenate([value[:, 8:16], value[:, 20:]], axis=1)
    out[:, :, :HALF] = jnp.swapaxes(left, 0, 1).astype(jnp.bfloat16)
    out[:, :, HALF:] = jnp.swapaxes(right, 0, 1).astype(jnp.bfloat16)


def orthogonal_rows(pieces):
    return call(
        orthogonal_kernel,
        jax.ShapeDtypeStruct(pieces[0].shape, jnp.bfloat16),
        *pieces,
        scratch=[
            pltpu.VMEM((FF, D), jnp.bfloat16),
            pltpu.VMEM((FF, FF), jnp.float32),
            pltpu.VMEM((FF, FF), jnp.bfloat16),
            pltpu.VMEM((FF, FF), jnp.bfloat16),
            pltpu.VMEM((FF, D), jnp.bfloat16),
        ],
        cost=pl.CostEstimate(
            flops=2 * FF * (3 * FF * D + FF * FF), bytes_accessed=2 * FF * D, transcendentals=0
        ),
    )


def exchanged(value, axes, groups=None):
    return lax.all_to_all(value, axes, split_axis=0, concat_axis=0, tiled=True, axis_index_groups=groups)


def gathered(piece):
    def across(value):
        return lax.ppermute(value, "z", [(plane, plane ^ 1) for plane in range(16)])

    pieces = [piece]
    for shift in SHIFTS:
        near = lax.ppermute(piece, "x", [(place, (place + shift) % 4) for place in range(4)])
        pieces += [near, across(near)]
    return pieces + [across(piece)]


def local(gradient, momentum):
    shape = (gradient.shape[1], MATS, D)
    gradient, momentum = jnp.swapaxes(gradient, 0, 1), jnp.swapaxes(momentum, 0, 1)
    whole = jax.ShapeDtypeStruct(shape, jnp.float32)
    squares, kept, decayed = call(
        start_kernel,
        (jax.ShapeDtypeStruct((32, 1, 128), jnp.float32), whole, whole),
        gradient,
        momentum,
        scratch=[pltpu.SemaphoreType.DMA((2,))],
        space=pl.ANY,
        limit=54272,
    )
    squares = exchanged(squares, ("x", "y", "core"))
    squares = call(add_kernel, jax.ShapeDtypeStruct((16, 1, 128), jnp.float32), squares)
    squares = exchanged(squares, "z")
    momentum_next, outgoing = call(
        blend_kernel,
        (
            whole,
            jax.ShapeDtypeStruct((MATS, 24, HALF), jnp.bfloat16),
        ),
        squares,
        kept,
        decayed,
    )
    piece = exchanged(outgoing, "z", PLANES)
    returning = orthogonal_rows(gathered(piece))
    arrived = exchanged(returning, "z", PLANES)
    update = call(spread_kernel, jax.ShapeDtypeStruct(shape, jnp.bfloat16), arrived)
    return (jnp.swapaxes(momentum_next, 0, 1), jnp.swapaxes(update, 0, 1))


def solution(mesh):
    split = Mesh(mesh.devices.reshape(16, 4, 4, 2), ("z", "x", "y", "core"))
    spec = P(("y", "core"), ("z", "x"), None)
    return jax.shard_map(local, mesh=split, in_specs=(spec, spec), out_specs=(spec, spec), check_vma=False)
```

```python
import math

import jax
import jax.numpy as jnp
from jax import lax
from jax.experimental import pallas as pl
from jax.experimental.pallas import tpu as pltpu
from jax.sharding import Mesh, PartitionSpec as P

D = 1024
FF = 768
MATS = 8
HALF = D // 2
TILE = 256
PLANES = ((0, 2, 4, 6, 9, 11, 13, 15), (1, 3, 5, 7, 8, 10, 12, 14))


MOMENTUM_RATE = 0.95
RMS_CAP = 0.5
NORM_EPS = 1e-07
COEF_A = 3.4445
COEF_B = -4.775
COEF_C = 2.0315


def dot_f32(left, right):
    return jnp.dot(left, right, preferred_element_type=jnp.float32)


def dot_transposed(left, right):
    return lax.dot_general(left, right, (((1,), (1,)), ((), ())), preferred_element_type=jnp.float32)


def call(kernel, out_shape, *args, scratch=(), cost=None, space=pltpu.VMEM, limit=32768):
    return pl.pallas_call(
        kernel,
        out_shape=out_shape,
        in_specs=[pl.BlockSpec(memory_space=space)] * len(args),
        out_specs=jax.tree.map(lambda _: pl.BlockSpec(memory_space=pltpu.VMEM), out_shape),
        scratch_shapes=scratch,
        compiler_params=pltpu.CompilerParams(vmem_limit_bytes=limit * 1024),
        cost_estimate=cost,
    )(*args)


def start_kernel(gradient, momentum, sums, kept, decayed, arrivals):
    copies = [
        pltpu.make_async_copy(gradient, kept, arrivals.at[0]),
        pltpu.make_async_copy(momentum, decayed, arrivals.at[1]),
    ]
    for copy in copies:
        copy.start()
    copies[0].wait()
    value = kept[...]
    sums[...] = jnp.broadcast_to(jnp.sum(value * value), sums.shape)
    copies[1].wait()
    decayed[...] = MOMENTUM_RATE * decayed[...]


def add_kernel(parts, out):
    out[...] = jnp.broadcast_to(jnp.sum(parts[...], axis=0, keepdims=True), out.shape)


def blend_kernel(total, gradient, decayed, momentum_next, outgoing):
    total_square = jnp.sum(total[...], axis=0)[:, :1]
    factor = jnp.minimum(1.0, RMS_CAP * math.sqrt(MATS * MATS * FF * D) / jnp.sqrt(total_square))
    scaled = factor[None] * gradient[...]
    following = decayed[...] + scaled
    momentum_next[...] = following
    blended = jnp.swapaxes(scaled + MOMENTUM_RATE * following, 0, 1)
    left, right = blended[:, :, :HALF], blended[:, :, HALF:]
    packed = jnp.concatenate([left[:, :8], right[:, :8], left[:, 8:], right[:, 8:]], axis=1)
    outgoing[...] = packed.astype(jnp.bfloat16)


def unpacked(value):
    left, right = [], []
    for number in range(0, MATS, 2):
        first, second = value[number], value[number + 1]
        left += [first[:8], second[:8], first[16:20], second[16:20]]
        right += [first[8:16], second[8:16], first[20:], second[20:]]
    return jnp.concatenate(left, axis=0), jnp.concatenate(right, axis=0)


def packed_blocks(left, right):
    blocks = []
    for start in range(0, left.shape[0], 24):
        for place in range(2):
            head, tail = start + 8 * place, start + 16 + 4 * place
            blocks.append(
                jnp.concatenate(
                    [left[head : head + 8], right[head : head + 8], left[tail : tail + 4], right[tail : tail + 4]],
                    axis=0,
                )
            )
    return blocks


def orthogonal_kernel(*refs):
    pieces, (out, whole, product, gram, poly, second) = refs[:MATS], refs[MATS:]
    rows = FF // MATS
    tiles = [slice(start, start + TILE) for start in range(0, FF, TILE)]
    for number, piece in enumerate(pieces):
        left, right = unpacked(piece[...].astype(jnp.float32))
        place = slice(number * rows, (number + 1) * rows)
        whole[place, :HALF] = left.astype(jnp.bfloat16)
        whole[place, HALF:] = right.astype(jnp.bfloat16)
    on_diagonal = lax.broadcasted_iota(jnp.int32, (TILE, TILE), 0) == lax.broadcasted_iota(
        jnp.int32, (TILE, TILE), 1
    )
    norm_square = jnp.float32(0.0)
    for tile in tiles:
        product[tile, :] = dot_transposed(whole[tile, :], whole[...])
        norm_square += jnp.sum(jnp.where(on_diagonal, product[tile, tile], 0.0))
    inverse = 1.0 / (jnp.sqrt(jnp.full((1, 1), norm_square, jnp.float32)) + NORM_EPS)
    for tile in tiles:
        gram[tile, :] = (product[tile, :] * (inverse * inverse)).astype(jnp.bfloat16)
    for tile in tiles:
        squared = dot_f32(gram[tile, :], gram[...])
        poly[tile, :] = (COEF_B * gram[tile, :].astype(jnp.float32) + COEF_C * squared).astype(
            jnp.bfloat16
        )
    for tile in tiles:
        combined = COEF_A * whole[tile, :].astype(jnp.float32) + dot_f32(poly[tile, :], whole[...])
        second[tile, :] = (inverse * combined).astype(jnp.bfloat16)
    for tile in tiles:
        gram[tile, :] = dot_transposed(second[tile, :], second[...]).astype(jnp.bfloat16)
    own = gram[:rows, :]
    own_poly = (COEF_B * own.astype(jnp.float32) + COEF_C * dot_f32(own, gram[...])).astype(
        jnp.bfloat16
    )
    combined = COEF_A * second[:rows, :].astype(jnp.float32) + dot_f32(own_poly, second[...])
    scaled = 0.2 * math.sqrt(max(FF, D)) * combined
    for number, block in enumerate(packed_blocks(scaled[:, :HALF], scaled[:, HALF:])):
        out[number] = block.astype(jnp.bfloat16)


def spread_kernel(arrived, out):
    value = arrived[...].astype(jnp.float32)
    left = jnp.concatenate([value[:, :8], value[:, 16:20]], axis=1)
    right = jnp.concatenate([value[:, 8:16], value[:, 20:]], axis=1)
    out[:, :, :HALF] = jnp.swapaxes(left, 0, 1).astype(jnp.bfloat16)
    out[:, :, HALF:] = jnp.swapaxes(right, 0, 1).astype(jnp.bfloat16)


def orthogonal_rows(pieces):
    return call(
        orthogonal_kernel,
        jax.ShapeDtypeStruct(pieces[0].shape, jnp.bfloat16),
        *pieces,
        scratch=[
            pltpu.VMEM((FF, D), jnp.bfloat16),
            pltpu.VMEM((FF, FF), jnp.float32),
            pltpu.VMEM((FF, FF), jnp.bfloat16),
            pltpu.VMEM((FF, FF), jnp.bfloat16),
            pltpu.VMEM((FF, D), jnp.bfloat16),
        ],
        cost=pl.CostEstimate(
            flops=2 * FF * (3 * FF * D + FF * FF), bytes_accessed=2 * FF * D, transcendentals=0
        ),
    )


def exchanged(value, axes, groups=None):
    return lax.all_to_all(value, axes, split_axis=0, concat_axis=0, tiled=True, axis_index_groups=groups)


def gathered(piece):
    def across(value):
        return lax.ppermute(value, "z", [(plane, plane ^ 1) for plane in range(16)])

    def along(value, shift):
        return lax.ppermute(value, "x", [(place, (place + shift) % 4) for place in range(4)])

    next_x, back_x, plane, far_x = along(piece, 1), along(piece, 3), across(piece), along(piece, 2)
    return [piece, next_x, back_x, across(back_x), plane, along(plane, 1), far_x, across(far_x)]


def local(gradient, momentum):
    shape = (gradient.shape[1], MATS, D)
    gradient, momentum = jnp.swapaxes(gradient, 0, 1), jnp.swapaxes(momentum, 0, 1)
    whole = jax.ShapeDtypeStruct(shape, jnp.float32)
    squares, kept, decayed = call(
        start_kernel,
        (jax.ShapeDtypeStruct((32, 1, 128), jnp.float32), whole, whole),
        gradient,
        momentum,
        scratch=[pltpu.SemaphoreType.DMA((2,))],
        space=pl.ANY,
        limit=54272,
    )
    squares = exchanged(squares, ("x", "y", "core"))
    squares = call(add_kernel, jax.ShapeDtypeStruct((16, 1, 128), jnp.float32), squares)
    squares = exchanged(squares, "z")
    momentum_next, outgoing = call(
        blend_kernel,
        (
            whole,
            jax.ShapeDtypeStruct((MATS, 24, HALF), jnp.bfloat16),
        ),
        squares,
        kept,
        decayed,
    )
    piece = exchanged(outgoing, "z", PLANES)
    returning = orthogonal_rows(gathered(piece))
    arrived = exchanged(returning, "z", PLANES)
    update = call(spread_kernel, jax.ShapeDtypeStruct(shape, jnp.bfloat16), arrived)
    return (jnp.swapaxes(momentum_next, 0, 1), jnp.swapaxes(update, 0, 1))


def solution(mesh):
    split = Mesh(mesh.devices.reshape(16, 4, 4, 2), ("z", "x", "y", "core"))
    spec = P(("y", "core"), ("z", "x"), None)
    return jax.shard_map(local, mesh=split, in_specs=(spec, spec), out_specs=(spec, spec), check_vma=False)
```

```python
import math

import jax
import jax.numpy as jnp
from jax import lax
from jax.experimental import pallas as pl
from jax.experimental.pallas import tpu as pltpu
from jax.sharding import Mesh, PartitionSpec as P

D = 1024
FF = 768
MATS = 8
HALF = D // 2
TILE = 256
PLANES = ((0, 2, 4, 6, 9, 11, 13, 15), (1, 3, 5, 7, 8, 10, 12, 14))


MOMENTUM_RATE = 0.95
RMS_CAP = 0.5
NORM_EPS = 1e-07
COEF_A = 3.4445
COEF_B = -4.775
COEF_C = 2.0315


def dot_f32(left, right):
    return jnp.dot(left, right, preferred_element_type=jnp.float32)


def dot_transposed(left, right):
    return lax.dot_general(left, right, (((1,), (1,)), ((), ())), preferred_element_type=jnp.float32)


def call(kernel, out_shape, *args, scratch=(), cost=None, space=pltpu.VMEM, limit=32768):
    return pl.pallas_call(
        kernel,
        out_shape=out_shape,
        in_specs=[pl.BlockSpec(memory_space=space)] * len(args),
        out_specs=jax.tree.map(lambda _: pl.BlockSpec(memory_space=pltpu.VMEM), out_shape),
        scratch_shapes=scratch,
        compiler_params=pltpu.CompilerParams(vmem_limit_bytes=limit * 1024),
        cost_estimate=cost,
    )(*args)


def start_kernel(gradient, momentum, sums, kept, decayed, arrivals):
    copies = [
        pltpu.make_async_copy(gradient, kept, arrivals.at[0]),
        pltpu.make_async_copy(momentum, decayed, arrivals.at[1]),
    ]
    for copy in copies:
        copy.start()
    copies[0].wait()
    value = kept[...]
    sums[...] = jnp.broadcast_to(jnp.sum(value * value), sums.shape)
    copies[1].wait()
    decayed[...] = MOMENTUM_RATE * decayed[...]


def add_kernel(parts, out):
    out[...] = jnp.broadcast_to(jnp.sum(parts[...], axis=0, keepdims=True), out.shape)


def blend_kernel(total, gradient, decayed, momentum_next, outgoing):
    total_square = jnp.sum(total[...], axis=0)[:, :1]
    factor = jnp.minimum(1.0, RMS_CAP * math.sqrt(MATS * MATS * FF * D) / jnp.sqrt(total_square))
    scaled = factor[None] * gradient[...]
    following = decayed[...] + scaled
    momentum_next[...] = following
    blended = jnp.swapaxes(scaled + MOMENTUM_RATE * following, 0, 1)
    left, right = blended[:, :, :HALF], blended[:, :, HALF:]
    packed = jnp.concatenate([left[:, :8], right[:, :8], left[:, 8:], right[:, 8:]], axis=1)
    outgoing[...] = packed.astype(jnp.bfloat16)


def unpacked(value):
    left, right = [], []
    for number in range(0, MATS, 2):
        first, second = value[number], value[number + 1]
        left += [first[:8], second[:8], first[16:20], second[16:20]]
        right += [first[8:16], second[8:16], first[20:], second[20:]]
    return jnp.concatenate(left, axis=0), jnp.concatenate(right, axis=0)


def packed_blocks(left, right):
    blocks = []
    for start in range(0, left.shape[0], 24):
        for place in range(2):
            head, tail = start + 8 * place, start + 16 + 4 * place
            blocks.append(
                jnp.concatenate(
                    [left[head : head + 8], right[head : head + 8], left[tail : tail + 4], right[tail : tail + 4]],
                    axis=0,
                )
            )
    return blocks


def orthogonal_kernel(*refs):
    pieces, (out, whole, product, gram, poly, second) = refs[:MATS], refs[MATS:]
    rows = FF // MATS
    tiles = [slice(start, start + TILE) for start in range(0, FF, TILE)]
    for number, piece in enumerate(pieces):
        left, right = unpacked(piece[...].astype(jnp.float32))
        place = slice(number * rows, (number + 1) * rows)
        whole[place, :HALF] = left.astype(jnp.bfloat16)
        whole[place, HALF:] = right.astype(jnp.bfloat16)
    on_diagonal = lax.broadcasted_iota(jnp.int32, (TILE, TILE), 0) == lax.broadcasted_iota(
        jnp.int32, (TILE, TILE), 1
    )
    norm_square = jnp.float32(0.0)
    for tile in tiles:
        product[tile, :] = dot_transposed(whole[tile, :], whole[...])
        norm_square += jnp.sum(jnp.where(on_diagonal, product[tile, tile], 0.0))
    inverse = 1.0 / (jnp.sqrt(jnp.full((1, 1), norm_square, jnp.float32)) + NORM_EPS)
    for tile in tiles:
        gram[tile, :] = (product[tile, :] * (inverse * inverse)).astype(jnp.bfloat16)
    for tile in tiles:
        squared = dot_f32(gram[tile, :], gram[...])
        poly[tile, :] = (COEF_B * gram[tile, :].astype(jnp.float32) + COEF_C * squared).astype(
            jnp.bfloat16
        )
    for tile in tiles:
        combined = COEF_A * whole[tile, :].astype(jnp.float32) + dot_f32(poly[tile, :], whole[...])
        second[tile, :] = (inverse * combined).astype(jnp.bfloat16)
    for tile in tiles:
        gram[tile, :] = dot_transposed(second[tile, :], second[...]).astype(jnp.bfloat16)
    own = gram[:rows, :]
    own_poly = (COEF_B * own.astype(jnp.float32) + COEF_C * dot_f32(own, gram[...])).astype(
        jnp.bfloat16
    )
    combined = COEF_A * second[:rows, :].astype(jnp.float32) + dot_f32(own_poly, second[...])
    scaled = 0.2 * math.sqrt(max(FF, D)) * combined
    for number, block in enumerate(packed_blocks(scaled[:, :HALF], scaled[:, HALF:])):
        out[number] = block.astype(jnp.bfloat16)


def spread_kernel(arrived, out):
    value = arrived[...].astype(jnp.float32)
    left = jnp.concatenate([value[:, :8], value[:, 16:20]], axis=1)
    right = jnp.concatenate([value[:, 8:16], value[:, 20:]], axis=1)
    out[:, :, :HALF] = jnp.swapaxes(left, 0, 1).astype(jnp.bfloat16)
    out[:, :, HALF:] = jnp.swapaxes(right, 0, 1).astype(jnp.bfloat16)


def orthogonal_rows(pieces):
    return call(
        orthogonal_kernel,
        jax.ShapeDtypeStruct(pieces[0].shape, jnp.bfloat16),
        *pieces,
        scratch=[
            pltpu.VMEM((FF, D), jnp.bfloat16),
            pltpu.VMEM((FF, FF), jnp.float32),
            pltpu.VMEM((FF, FF), jnp.bfloat16),
            pltpu.VMEM((FF, FF), jnp.bfloat16),
            pltpu.VMEM((FF, D), jnp.bfloat16),
        ],
        cost=pl.CostEstimate(
            flops=2 * FF * (3 * FF * D + FF * FF), bytes_accessed=2 * FF * D, transcendentals=0
        ),
    )


def exchanged(value, axes, groups=None):
    return lax.all_to_all(value, axes, split_axis=0, concat_axis=0, tiled=True, axis_index_groups=groups)


def gathered(piece):
    def swapped(value, axis, flip):
        size = lax.axis_size(axis)
        return lax.ppermute(value, axis, [(place, place ^ flip) for place in range(size)])

    side, other_side, far = swapped(piece, "x", 1), swapped(piece, "x", 3), swapped(piece, "x", 2)
    plane = swapped(piece, "z", 1)
    return [
        piece,
        side,
        other_side,
        far,
        swapped(far, "z", 1),
        plane,
        swapped(plane, "x", 3),
        swapped(plane, "x", 1),
    ]


def local(gradient, momentum):
    shape = (gradient.shape[1], MATS, D)
    gradient, momentum = jnp.swapaxes(gradient, 0, 1), jnp.swapaxes(momentum, 0, 1)
    whole = jax.ShapeDtypeStruct(shape, jnp.float32)
    squares, kept, decayed = call(
        start_kernel,
        (jax.ShapeDtypeStruct((32, 1, 128), jnp.float32), whole, whole),
        gradient,
        momentum,
        scratch=[pltpu.SemaphoreType.DMA((2,))],
        space=pl.ANY,
        limit=54272,
    )
    squares = exchanged(squares, ("x", "y", "core"))
    squares = call(add_kernel, jax.ShapeDtypeStruct((16, 1, 128), jnp.float32), squares)
    squares = exchanged(squares, "z")
    momentum_next, outgoing = call(
        blend_kernel,
        (
            whole,
            jax.ShapeDtypeStruct((MATS, 24, HALF), jnp.bfloat16),
        ),
        squares,
        kept,
        decayed,
    )
    piece = exchanged(outgoing, "z", PLANES)
    returning = orthogonal_rows(gathered(piece))
    arrived = exchanged(returning, "z", PLANES)
    update = call(spread_kernel, jax.ShapeDtypeStruct(shape, jnp.bfloat16), arrived)
    return (jnp.swapaxes(momentum_next, 0, 1), jnp.swapaxes(update, 0, 1))


def solution(mesh):
    split = Mesh(mesh.devices.reshape(16, 4, 4, 2), ("z", "x", "y", "core"))
    spec = P(("y", "core"), ("z", "x"), None)
    return jax.shard_map(local, mesh=split, in_specs=(spec, spec), out_specs=(spec, spec), check_vma=False)
```

```python
import math

import jax
import jax.numpy as jnp
from jax import lax
from jax.experimental import pallas as pl
from jax.experimental.pallas import tpu as pltpu
from jax.sharding import Mesh, PartitionSpec as P

D = 1024
FF = 768
MATS = 8
HALF = D // 2
TILE = 256
PLANES = ((0, 2, 4, 6, 9, 11, 13, 15), (1, 3, 5, 7, 8, 10, 12, 14))


MOMENTUM_RATE = 0.95
RMS_CAP = 0.5
NORM_EPS = 1e-07
COEF_A = 3.4445
COEF_B = -4.775
COEF_C = 2.0315


def dot_f32(left, right):
    return jnp.dot(left, right, preferred_element_type=jnp.float32)


def dot_transposed(left, right):
    return lax.dot_general(left, right, (((1,), (1,)), ((), ())), preferred_element_type=jnp.float32)


def call(kernel, out_shape, *args, scratch=(), cost=None, space=pltpu.VMEM, limit=32768):
    return pl.pallas_call(
        kernel,
        out_shape=out_shape,
        in_specs=[pl.BlockSpec(memory_space=space)] * len(args),
        out_specs=jax.tree.map(lambda _: pl.BlockSpec(memory_space=pltpu.VMEM), out_shape),
        scratch_shapes=scratch,
        compiler_params=pltpu.CompilerParams(vmem_limit_bytes=limit * 1024),
        cost_estimate=cost,
    )(*args)


def start_kernel(gradient, momentum, sums, kept, decayed, arrivals):
    copies = [
        pltpu.make_async_copy(gradient, kept, arrivals.at[0]),
        pltpu.make_async_copy(momentum, decayed, arrivals.at[1]),
    ]
    for copy in copies:
        copy.start()
    copies[0].wait()
    value = kept[...]
    sums[...] = jnp.broadcast_to(jnp.sum(value * value), sums.shape)
    copies[1].wait()
    decayed[...] = MOMENTUM_RATE * decayed[...]


def add_kernel(parts, out):
    out[...] = jnp.broadcast_to(jnp.sum(parts[...], axis=0, keepdims=True), out.shape)


def factor_of(total):
    total_square = jnp.sum(total[...], axis=0)[:, :1]
    factor = jnp.minimum(1.0, RMS_CAP * math.sqrt(MATS * MATS * FF * D) / jnp.sqrt(total_square))
    return factor[None]


def follow_kernel(total, gradient, decayed, momentum_next):
    momentum_next[...] = decayed[...] + factor_of(total) * gradient[...]


def blend_kernel(total, gradient, decayed, outgoing):
    scaled = factor_of(total) * gradient[...]
    blended = jnp.swapaxes(scaled + MOMENTUM_RATE * (decayed[...] + scaled), 0, 1)
    left, right = blended[:, :, :HALF], blended[:, :, HALF:]
    packed = jnp.concatenate([left[:, :8], right[:, :8], left[:, 8:], right[:, 8:]], axis=1)
    outgoing[...] = packed.astype(jnp.bfloat16)


def unpacked(value):
    left, right = [], []
    for number in range(0, MATS, 2):
        first, second = value[number], value[number + 1]
        left += [first[:8], second[:8], first[16:20], second[16:20]]
        right += [first[8:16], second[8:16], first[20:], second[20:]]
    return jnp.concatenate(left, axis=0), jnp.concatenate(right, axis=0)


def packed_blocks(left, right):
    blocks = []
    for start in range(0, left.shape[0], 24):
        for place in range(2):
            head, tail = start + 8 * place, start + 16 + 4 * place
            blocks.append(
                jnp.concatenate(
                    [left[head : head + 8], right[head : head + 8], left[tail : tail + 4], right[tail : tail + 4]],
                    axis=0,
                )
            )
    return blocks


def orthogonal_kernel(*refs):
    pieces, (out, whole, gram, poly, second) = refs[:MATS], refs[MATS:]
    rows = FF // MATS
    tiles = [slice(start, start + TILE) for start in range(0, FF, TILE)]
    squares = jnp.zeros(pieces[0].shape[1:], jnp.float32)
    for number, piece in enumerate(pieces):
        value = piece[...].astype(jnp.float32)
        squares += jnp.sum(value * value, axis=0)
        left, right = unpacked(value)
        place = slice(number * rows, (number + 1) * rows)
        whole[place, :HALF] = left.astype(jnp.bfloat16)
        whole[place, HALF:] = right.astype(jnp.bfloat16)
    norm_square = jnp.full((1, 1), jnp.sum(squares), jnp.float32)
    inverse = 1.0 / (jnp.sqrt(norm_square) + NORM_EPS)
    for tile in tiles:
        product = dot_transposed(whole[tile, :], whole[...])
        gram[tile, :] = (product * (inverse * inverse)).astype(jnp.bfloat16)
    for tile in tiles:
        squared = dot_f32(gram[tile, :], gram[...])
        poly[tile, :] = (COEF_B * gram[tile, :].astype(jnp.float32) + COEF_C * squared).astype(
            jnp.bfloat16
        )
    for tile in tiles:
        combined = COEF_A * whole[tile, :].astype(jnp.float32) + dot_f32(poly[tile, :], whole[...])
        second[tile, :] = (inverse * combined).astype(jnp.bfloat16)
    for tile in tiles:
        gram[tile, :] = dot_transposed(second[tile, :], second[...]).astype(jnp.bfloat16)
    own = gram[:rows, :]
    own_poly = (COEF_B * own.astype(jnp.float32) + COEF_C * dot_f32(own, gram[...])).astype(
        jnp.bfloat16
    )
    combined = COEF_A * second[:rows, :].astype(jnp.float32) + dot_f32(own_poly, second[...])
    scaled = 0.2 * math.sqrt(max(FF, D)) * combined
    for number, block in enumerate(packed_blocks(scaled[:, :HALF], scaled[:, HALF:])):
        out[number] = block.astype(jnp.bfloat16)


def spread_kernel(arrived, out):
    value = arrived[...].astype(jnp.float32)
    left = jnp.concatenate([value[:, :8], value[:, 16:20]], axis=1)
    right = jnp.concatenate([value[:, 8:16], value[:, 20:]], axis=1)
    out[:, :, :HALF] = jnp.swapaxes(left, 0, 1).astype(jnp.bfloat16)
    out[:, :, HALF:] = jnp.swapaxes(right, 0, 1).astype(jnp.bfloat16)


def orthogonal_rows(pieces):
    return call(
        orthogonal_kernel,
        jax.ShapeDtypeStruct(pieces[0].shape, jnp.bfloat16),
        *pieces,
        scratch=[
            pltpu.VMEM((FF, D), jnp.bfloat16),
            pltpu.VMEM((FF, FF), jnp.bfloat16),
            pltpu.VMEM((FF, FF), jnp.bfloat16),
            pltpu.VMEM((FF, D), jnp.bfloat16),
        ],
        cost=pl.CostEstimate(
            flops=2 * FF * (3 * FF * D + FF * FF), bytes_accessed=2 * FF * D, transcendentals=0
        ),
    )


def exchanged(value, axes, groups=None):
    return lax.all_to_all(value, axes, split_axis=0, concat_axis=0, tiled=True, axis_index_groups=groups)


def gathered(piece):
    def swapped(value, axis, flip):
        size = lax.axis_size(axis)
        return lax.ppermute(value, axis, [(place, place ^ flip) for place in range(size)])

    side, other_side, far = swapped(piece, "x", 1), swapped(piece, "x", 3), swapped(piece, "x", 2)
    plane = swapped(piece, "z", 1)
    return [
        piece,
        side,
        other_side,
        far,
        swapped(far, "z", 1),
        plane,
        swapped(plane, "x", 3),
        swapped(plane, "x", 1),
    ]


def local(gradient, momentum):
    shape = (gradient.shape[1], MATS, D)
    gradient, momentum = jnp.swapaxes(gradient, 0, 1), jnp.swapaxes(momentum, 0, 1)
    whole = jax.ShapeDtypeStruct(shape, jnp.float32)
    squares, kept, decayed = call(
        start_kernel,
        (jax.ShapeDtypeStruct((32, 1, 128), jnp.float32), whole, whole),
        gradient,
        momentum,
        scratch=[pltpu.SemaphoreType.DMA((2,))],
        space=pl.ANY,
        limit=54272,
    )
    squares = exchanged(squares, ("x", "y", "core"))
    squares = call(add_kernel, jax.ShapeDtypeStruct((16, 1, 128), jnp.float32), squares)
    squares = exchanged(squares, "z")
    outgoing = call(
        blend_kernel, jax.ShapeDtypeStruct((MATS, 24, HALF), jnp.bfloat16), squares, kept, decayed
    )
    piece = exchanged(outgoing, "z", PLANES)
    returning = orthogonal_rows(gathered(piece))
    momentum_next = call(follow_kernel, whole, squares, kept, decayed)
    arrived = exchanged(returning, "z", PLANES)
    update = call(spread_kernel, jax.ShapeDtypeStruct(shape, jnp.bfloat16), arrived)
    return (jnp.swapaxes(momentum_next, 0, 1), jnp.swapaxes(update, 0, 1))


def solution(mesh):
    split = Mesh(mesh.devices.reshape(16, 4, 4, 2), ("z", "x", "y", "core"))
    spec = P(("y", "core"), ("z", "x"), None)
    return jax.shard_map(local, mesh=split, in_specs=(spec, spec), out_specs=(spec, spec), check_vma=False)
```

```python
import itertools
import math

import jax
import jax.numpy as jnp
from jax import lax
from jax.experimental import pallas as pl
from jax.experimental.pallas import tpu as pltpu
from jax.sharding import Mesh, PartitionSpec as P

D = 1024
FF = 768
MATS = 8
HALF = D // 2
TILE = 256
PLANES = ((0, 2, 4, 6, 9, 11, 13, 15), (1, 3, 5, 7, 8, 10, 12, 14))


MOMENTUM_RATE = 0.95
RMS_CAP = 0.5
NORM_EPS = 1e-07
COEF_A = 3.4445
COEF_B = -4.775
COEF_C = 2.0315


def dot_f32(left, right):
    return jnp.dot(left, right, preferred_element_type=jnp.float32)


def dot_transposed(left, right):
    return lax.dot_general(left, right, (((1,), (1,)), ((), ())), preferred_element_type=jnp.float32)


def call(kernel, out_shape, *args, scratch=(), cost=None, space=pltpu.VMEM, limit=32768):
    return pl.pallas_call(
        kernel,
        out_shape=out_shape,
        in_specs=[pl.BlockSpec(memory_space=space)] * len(args),
        out_specs=jax.tree.map(lambda _: pl.BlockSpec(memory_space=pltpu.VMEM), out_shape),
        scratch_shapes=scratch,
        compiler_params=pltpu.CompilerParams(vmem_limit_bytes=limit * 1024),
        cost_estimate=cost,
    )(*args)


def start_kernel(gradient, momentum, sums, kept, decayed, arrivals):
    copies = [
        pltpu.make_async_copy(gradient, kept, arrivals.at[0]),
        pltpu.make_async_copy(momentum, decayed, arrivals.at[1]),
    ]
    for copy in copies:
        copy.start()
    copies[0].wait()
    value = kept[...]
    sums[...] = jnp.broadcast_to(jnp.sum(value * value), sums.shape)
    copies[1].wait()
    decayed[...] = MOMENTUM_RATE * decayed[...]


def add_kernel(parts, out):
    out[...] = jnp.broadcast_to(jnp.sum(parts[...], axis=0, keepdims=True), out.shape)


def factor_of(total):
    total_square = jnp.sum(total[...], axis=0)[:, :1]
    factor = jnp.minimum(1.0, RMS_CAP * math.sqrt(MATS * MATS * FF * D) / jnp.sqrt(total_square))
    return factor[None]


def follow_kernel(total, gradient, decayed, momentum_next):
    momentum_next[...] = decayed[...] + factor_of(total) * gradient[...]


def blend_kernel(total, gradient, decayed, outgoing):
    scaled = factor_of(total) * gradient[...]
    blended = jnp.swapaxes(scaled + MOMENTUM_RATE * (decayed[...] + scaled), 0, 1)
    left, right = blended[:, :, :HALF], blended[:, :, HALF:]
    packed = jnp.concatenate([left[:, :8], right[:, :8], left[:, 8:], right[:, 8:]], axis=1)
    outgoing[...] = packed.astype(jnp.bfloat16)


def unpacked(value):
    left, right = [], []
    for number in range(0, MATS, 2):
        first, second = value[number], value[number + 1]
        left += [first[:8], second[:8], first[16:20], second[16:20]]
        right += [first[8:16], second[8:16], first[20:], second[20:]]
    return jnp.concatenate(left, axis=0), jnp.concatenate(right, axis=0)


def packed_blocks(left, right):
    blocks = []
    for start in range(0, left.shape[0], 24):
        for place in range(2):
            head, tail = start + 8 * place, start + 16 + 4 * place
            blocks.append(
                jnp.concatenate(
                    [left[head : head + 8], right[head : head + 8], left[tail : tail + 4], right[tail : tail + 4]],
                    axis=0,
                )
            )
    return blocks


def orthogonal_kernel(*refs):
    pieces, (out, whole, gram, poly, second) = refs[:MATS], refs[MATS:]
    rows = FF // MATS
    tiles = [slice(start, start + TILE) for start in range(0, FF, TILE)]
    squares = jnp.zeros(pieces[0].shape[1:], jnp.float32)
    for number, piece in enumerate(pieces):
        value = piece[...].astype(jnp.float32)
        squares += jnp.sum(value * value, axis=0)
        left, right = unpacked(value)
        place = slice(number * rows, (number + 1) * rows)
        whole[place, :HALF] = left.astype(jnp.bfloat16)
        whole[place, HALF:] = right.astype(jnp.bfloat16)
    norm_square = jnp.full((1, 1), jnp.sum(squares), jnp.float32)
    inverse = 1.0 / (jnp.sqrt(norm_square) + NORM_EPS)
    for tile in tiles:
        product = dot_transposed(whole[tile, :], whole[...])
        gram[tile, :] = (product * (inverse * inverse)).astype(jnp.bfloat16)
    for tile in tiles:
        squared = dot_f32(gram[tile, :], gram[...])
        poly[tile, :] = (COEF_B * gram[tile, :].astype(jnp.float32) + COEF_C * squared).astype(
            jnp.bfloat16
        )
    for tile in tiles:
        combined = COEF_A * whole[tile, :].astype(jnp.float32) + dot_f32(poly[tile, :], whole[...])
        second[tile, :] = (inverse * combined).astype(jnp.bfloat16)
    for tile in tiles:
        gram[tile, :] = dot_transposed(second[tile, :], second[...]).astype(jnp.bfloat16)
    own = gram[:rows, :]
    own_poly = (COEF_B * own.astype(jnp.float32) + COEF_C * dot_f32(own, gram[...])).astype(
        jnp.bfloat16
    )
    combined = COEF_A * second[:rows, :].astype(jnp.float32) + dot_f32(own_poly, second[...])
    scaled = 0.2 * math.sqrt(max(FF, D)) * combined
    for number, block in enumerate(packed_blocks(scaled[:, :HALF], scaled[:, HALF:])):
        out[number] = block.astype(jnp.bfloat16)


def spread_kernel(arrived, out):
    value = arrived[...].astype(jnp.float32)
    left = jnp.concatenate([value[:, :8], value[:, 16:20]], axis=1)
    right = jnp.concatenate([value[:, 8:16], value[:, 20:]], axis=1)
    out[:, :, :HALF] = jnp.swapaxes(left, 0, 1).astype(jnp.bfloat16)
    out[:, :, HALF:] = jnp.swapaxes(right, 0, 1).astype(jnp.bfloat16)


def orthogonal_rows(pieces):
    return call(
        orthogonal_kernel,
        jax.ShapeDtypeStruct(pieces[0].shape, jnp.bfloat16),
        *pieces,
        scratch=[
            pltpu.VMEM((FF, D), jnp.bfloat16),
            pltpu.VMEM((FF, FF), jnp.bfloat16),
            pltpu.VMEM((FF, FF), jnp.bfloat16),
            pltpu.VMEM((FF, D), jnp.bfloat16),
        ],
        cost=pl.CostEstimate(
            flops=2 * FF * (3 * FF * D + FF * FF), bytes_accessed=2 * FF * D, transcendentals=0
        ),
    )


def exchanged(value, axes, groups=None):
    return lax.all_to_all(value, axes, split_axis=0, concat_axis=0, tiled=True, axis_index_groups=groups)


def swapped(value, flips):
    pairs = []
    for plane, place, core in itertools.product(range(16), range(4), range(2)):
        over, along = flips[core]
        target = ((plane ^ over) * 4 + (place ^ along)) * 2 + core
        pairs.append(((plane * 4 + place) * 2 + core, target))
    return lax.ppermute(value, ("z", "x", "core"), pairs)


def gathered(piece):
    first = swapped(piece, ((1, 0), (0, 1)))
    second = swapped(piece, ((0, 1), (1, 0)))
    third = swapped(piece, ((0, 2), (0, 3)))
    fourth = swapped(piece, ((0, 3), (0, 2)))
    return [
        piece,
        fourth,
        third,
        swapped(third, ((1, 0), (1, 0))),
        second,
        swapped(second, ((1, 0), (0, 2))),
        first,
        swapped(first, ((0, 3), (1, 0))),
    ]


def local(gradient, momentum):
    shape = (gradient.shape[1], MATS, D)
    gradient, momentum = jnp.swapaxes(gradient, 0, 1), jnp.swapaxes(momentum, 0, 1)
    whole = jax.ShapeDtypeStruct(shape, jnp.float32)
    squares, kept, decayed = call(
        start_kernel,
        (jax.ShapeDtypeStruct((32, 1, 128), jnp.float32), whole, whole),
        gradient,
        momentum,
        scratch=[pltpu.SemaphoreType.DMA((2,))],
        space=pl.ANY,
        limit=54272,
    )
    squares = exchanged(squares, ("x", "y", "core"))
    squares = call(add_kernel, jax.ShapeDtypeStruct((16, 1, 128), jnp.float32), squares)
    squares = exchanged(squares, "z")
    outgoing = call(
        blend_kernel, jax.ShapeDtypeStruct((MATS, 24, HALF), jnp.bfloat16), squares, kept, decayed
    )
    piece = exchanged(outgoing, "z", PLANES)
    returning = orthogonal_rows(gathered(piece))
    momentum_next = call(follow_kernel, whole, squares, kept, decayed)
    arrived = exchanged(returning, "z", PLANES)
    update = call(spread_kernel, jax.ShapeDtypeStruct(shape, jnp.bfloat16), arrived)
    return (jnp.swapaxes(momentum_next, 0, 1), jnp.swapaxes(update, 0, 1))


def solution(mesh):
    split = Mesh(mesh.devices.reshape(16, 4, 4, 2), ("z", "x", "y", "core"))
    spec = P(("y", "core"), ("z", "x"), None)
    return jax.shard_map(local, mesh=split, in_specs=(spec, spec), out_specs=(spec, spec), check_vma=False)
```

```python
import math

import jax
import jax.numpy as jnp
from jax import lax
from jax.experimental import pallas as pl
from jax.experimental.pallas import tpu as pltpu
from jax.sharding import Mesh, PartitionSpec as P

D = 1024
FF = 768
MATS = 8
HALF = D // 2
TILE = 256
PLANES = ((0, 2, 4, 6, 9, 11, 13, 15), (1, 3, 5, 7, 8, 10, 12, 14))


MOMENTUM_RATE = 0.95
RMS_CAP = 0.5
NORM_EPS = 1e-07
COEF_A = 3.4445
COEF_B = -4.775
COEF_C = 2.0315


def dot_f32(left, right):
    return jnp.dot(left, right, preferred_element_type=jnp.float32)


def dot_transposed(left, right):
    return lax.dot_general(left, right, (((1,), (1,)), ((), ())), preferred_element_type=jnp.float32)


def call(kernel, out_shape, *args, scratch=(), cost=None, space=pltpu.VMEM, limit=32768):
    return pl.pallas_call(
        kernel,
        out_shape=out_shape,
        in_specs=[pl.BlockSpec(memory_space=space)] * len(args),
        out_specs=jax.tree.map(lambda _: pl.BlockSpec(memory_space=pltpu.VMEM), out_shape),
        scratch_shapes=scratch,
        compiler_params=pltpu.CompilerParams(vmem_limit_bytes=limit * 1024),
        cost_estimate=cost,
    )(*args)


def start_kernel(gradient, momentum, sums, kept, decayed, arrivals):
    copies = [
        pltpu.make_async_copy(gradient, kept, arrivals.at[0]),
        pltpu.make_async_copy(momentum, decayed, arrivals.at[1]),
    ]
    for copy in copies:
        copy.start()
    copies[0].wait()
    value = kept[...]
    sums[...] = jnp.broadcast_to(jnp.sum(value * value), sums.shape)
    copies[1].wait()
    decayed[...] = MOMENTUM_RATE * decayed[...]


def add_kernel(parts, out):
    out[...] = jnp.broadcast_to(jnp.sum(parts[...], axis=0, keepdims=True), out.shape)


def factor_of(total):
    total_square = jnp.sum(total[...], axis=0)[:, :1]
    factor = jnp.minimum(1.0, RMS_CAP * math.sqrt(MATS * MATS * FF * D) / jnp.sqrt(total_square))
    return factor[None]


def follow_kernel(total, gradient, decayed, momentum_next):
    momentum_next[...] = decayed[...] + factor_of(total) * gradient[...]


def blend_kernel(total, gradient, decayed, outgoing):
    scaled = factor_of(total) * gradient[...]
    blended = jnp.swapaxes(scaled + MOMENTUM_RATE * (decayed[...] + scaled), 0, 1)
    left, right = blended[:, :, :HALF], blended[:, :, HALF:]
    packed = jnp.concatenate([left[:, :8], right[:, :8], left[:, 8:], right[:, 8:]], axis=1)
    outgoing[...] = packed.astype(jnp.bfloat16)


def unpacked(value):
    left, right = [], []
    for number in range(0, MATS, 2):
        first, second = value[number], value[number + 1]
        left += [first[:8], second[:8], first[16:20], second[16:20]]
        right += [first[8:16], second[8:16], first[20:], second[20:]]
    return jnp.concatenate(left, axis=0), jnp.concatenate(right, axis=0)


def packed_blocks(left, right):
    blocks = []
    for start in range(0, left.shape[0], 24):
        for place in range(2):
            head, tail = start + 8 * place, start + 16 + 4 * place
            blocks.append(
                jnp.concatenate(
                    [left[head : head + 8], right[head : head + 8], left[tail : tail + 4], right[tail : tail + 4]],
                    axis=0,
                )
            )
    return blocks


def orthogonal_kernel(*refs):
    pieces, (out, whole, product, gram, poly, second) = refs[:MATS], refs[MATS:]
    rows = FF // MATS
    tiles = [slice(start, start + TILE) for start in range(0, FF, TILE)]
    for number, piece in enumerate(pieces):
        left, right = unpacked(piece[...].astype(jnp.float32))
        place = slice(number * rows, (number + 1) * rows)
        whole[place, :HALF] = left.astype(jnp.bfloat16)
        whole[place, HALF:] = right.astype(jnp.bfloat16)
    on_diagonal = lax.broadcasted_iota(jnp.int32, (TILE, TILE), 0) == lax.broadcasted_iota(
        jnp.int32, (TILE, TILE), 1
    )
    norm_square = jnp.float32(0.0)
    for tile in tiles:
        product[tile, :] = dot_transposed(whole[tile, :], whole[...])
        norm_square += jnp.sum(jnp.where(on_diagonal, product[tile, tile], 0.0))
    inverse = 1.0 / (jnp.sqrt(jnp.full((1, 1), norm_square, jnp.float32)) + NORM_EPS)
    for tile in tiles:
        gram[tile, :] = (product[tile, :] * (inverse * inverse)).astype(jnp.bfloat16)
    for tile in tiles:
        squared = dot_f32(gram[tile, :], gram[...])
        poly[tile, :] = (COEF_B * gram[tile, :].astype(jnp.float32) + COEF_C * squared).astype(
            jnp.bfloat16
        )
    for tile in tiles:
        combined = COEF_A * whole[tile, :].astype(jnp.float32) + dot_f32(poly[tile, :], whole[...])
        second[tile, :] = (inverse * combined).astype(jnp.bfloat16)
    for tile in tiles:
        gram[tile, :] = dot_transposed(second[tile, :], second[...]).astype(jnp.bfloat16)
    own = gram[:rows, :]
    own_poly = (COEF_B * own.astype(jnp.float32) + COEF_C * dot_f32(own, gram[...])).astype(
        jnp.bfloat16
    )
    combined = COEF_A * second[:rows, :].astype(jnp.float32) + dot_f32(own_poly, second[...])
    scaled = 0.2 * math.sqrt(max(FF, D)) * combined
    for number, block in enumerate(packed_blocks(scaled[:, :HALF], scaled[:, HALF:])):
        out[number] = block.astype(jnp.bfloat16)


def spread_kernel(arrived, out):
    value = arrived[...].astype(jnp.float32)
    left = jnp.concatenate([value[:, :8], value[:, 16:20]], axis=1)
    right = jnp.concatenate([value[:, 8:16], value[:, 20:]], axis=1)
    out[:, :, :HALF] = jnp.swapaxes(left, 0, 1).astype(jnp.bfloat16)
    out[:, :, HALF:] = jnp.swapaxes(right, 0, 1).astype(jnp.bfloat16)


def orthogonal_rows(pieces):
    return call(
        orthogonal_kernel,
        jax.ShapeDtypeStruct(pieces[0].shape, jnp.bfloat16),
        *pieces,
        scratch=[
            pltpu.VMEM((FF, D), jnp.bfloat16),
            pltpu.VMEM((FF, FF), jnp.float32),
            pltpu.VMEM((FF, FF), jnp.bfloat16),
            pltpu.VMEM((FF, FF), jnp.bfloat16),
            pltpu.VMEM((FF, D), jnp.bfloat16),
        ],
        cost=pl.CostEstimate(
            flops=2 * FF * (3 * FF * D + FF * FF), bytes_accessed=2 * FF * D, transcendentals=0
        ),
    )


def exchanged(value, axes, groups=None):
    return lax.all_to_all(value, axes, split_axis=0, concat_axis=0, tiled=True, axis_index_groups=groups)


def gathered(piece):
    def swapped(value, axis, flip):
        size = lax.axis_size(axis)
        return lax.ppermute(value, axis, [(place, place ^ flip) for place in range(size)])

    plane, side, other_side = swapped(piece, "z", 1), swapped(piece, "x", 1), swapped(piece, "x", 3)
    far = swapped(side, "x", 3)
    return [
        piece,
        other_side,
        swapped(other_side, "z", 1),
        plane,
        swapped(plane, "x", 1),
        side,
        far,
        swapped(far, "z", 1),
    ]


def local(gradient, momentum):
    shape = (gradient.shape[1], MATS, D)
    gradient, momentum = jnp.swapaxes(gradient, 0, 1), jnp.swapaxes(momentum, 0, 1)
    whole = jax.ShapeDtypeStruct(shape, jnp.float32)
    squares, kept, decayed = call(
        start_kernel,
        (jax.ShapeDtypeStruct((32, 1, 128), jnp.float32), whole, whole),
        gradient,
        momentum,
        scratch=[pltpu.SemaphoreType.DMA((2,))],
        space=pl.ANY,
        limit=54272,
    )
    squares = exchanged(squares, ("x", "y", "core"))
    squares = call(add_kernel, jax.ShapeDtypeStruct((16, 1, 128), jnp.float32), squares)
    squares = exchanged(squares, "z")
    outgoing = call(
        blend_kernel, jax.ShapeDtypeStruct((MATS, 24, HALF), jnp.bfloat16), squares, kept, decayed
    )
    piece = exchanged(outgoing, "z", PLANES)
    returning = orthogonal_rows(gathered(piece))
    momentum_next = call(follow_kernel, whole, squares, kept, decayed)
    arrived = exchanged(returning, "z", PLANES)
    update = call(spread_kernel, jax.ShapeDtypeStruct(shape, jnp.bfloat16), arrived)
    return (jnp.swapaxes(momentum_next, 0, 1), jnp.swapaxes(update, 0, 1))


def solution(mesh):
    split = Mesh(mesh.devices.reshape(16, 4, 4, 2), ("z", "x", "y", "core"))
    spec = P(("y", "core"), ("z", "x"), None)
    return jax.shard_map(local, mesh=split, in_specs=(spec, spec), out_specs=(spec, spec), check_vma=False)
```

```python
import math

import jax
import jax.numpy as jnp
from jax import lax
from jax.experimental import pallas as pl
from jax.experimental.pallas import tpu as pltpu
from jax.sharding import Mesh, PartitionSpec as P

D = 1024
FF = 768
MATS = 8
HALF = D // 2
TILE = 256
PLANES = ((0, 2, 4, 6, 9, 11, 13, 15), (1, 3, 5, 7, 8, 10, 12, 14))


MOMENTUM_RATE = 0.95
RMS_CAP = 0.5
NORM_EPS = 1e-07
COEF_A = 3.4445
COEF_B = -4.775
COEF_C = 2.0315


def dot_f32(left, right):
    return jnp.dot(left, right, preferred_element_type=jnp.float32)


def dot_transposed(left, right):
    return lax.dot_general(left, right, (((1,), (1,)), ((), ())), preferred_element_type=jnp.float32)


def call(kernel, out_shape, *args, scratch=(), cost=None, space=pltpu.VMEM, limit=32768):
    return pl.pallas_call(
        kernel,
        out_shape=out_shape,
        in_specs=[pl.BlockSpec(memory_space=space)] * len(args),
        out_specs=jax.tree.map(lambda _: pl.BlockSpec(memory_space=pltpu.VMEM), out_shape),
        scratch_shapes=scratch,
        compiler_params=pltpu.CompilerParams(vmem_limit_bytes=limit * 1024),
        cost_estimate=cost,
    )(*args)


def start_kernel(gradient, momentum, sums, kept, decayed, arrivals):
    copies = [
        pltpu.make_async_copy(gradient, kept, arrivals.at[0]),
        pltpu.make_async_copy(momentum, decayed, arrivals.at[1]),
    ]
    for copy in copies:
        copy.start()
    copies[0].wait()
    value = kept[...]
    sums[...] = jnp.broadcast_to(jnp.sum(value * value), sums.shape)
    copies[1].wait()
    decayed[...] = MOMENTUM_RATE * decayed[...]


def add_kernel(parts, out):
    out[...] = jnp.broadcast_to(jnp.sum(parts[...], axis=0, keepdims=True), out.shape)


def factor_of(total):
    total_square = jnp.sum(total[...], axis=0)[:, :1]
    factor = jnp.minimum(1.0, RMS_CAP * math.sqrt(MATS * MATS * FF * D) / jnp.sqrt(total_square))
    return factor[None]


def follow_kernel(total, gradient, decayed, momentum_next, stamp):
    momentum_next[...] = decayed[...] + factor_of(total) * gradient[...]
    stamp[...] = jnp.sum(total[...], axis=0)


def blend_kernel(total, gradient, decayed, outgoing):
    scaled = factor_of(total) * gradient[...]
    blended = jnp.swapaxes(scaled + MOMENTUM_RATE * (decayed[...] + scaled), 0, 1)
    left, right = blended[:, :, :HALF], blended[:, :, HALF:]
    packed = jnp.concatenate([left[:, :8], right[:, :8], left[:, 8:], right[:, 8:]], axis=1)
    outgoing[...] = packed.astype(jnp.bfloat16)


def unpacked(value):
    left, right = [], []
    for number in range(0, MATS, 2):
        first, second = value[number], value[number + 1]
        left += [first[:8], second[:8], first[16:20], second[16:20]]
        right += [first[8:16], second[8:16], first[20:], second[20:]]
    return jnp.concatenate(left, axis=0), jnp.concatenate(right, axis=0)


def packed_blocks(left, right):
    blocks = []
    for start in range(0, left.shape[0], 24):
        for place in range(2):
            head, tail = start + 8 * place, start + 16 + 4 * place
            blocks.append(
                jnp.concatenate(
                    [left[head : head + 8], right[head : head + 8], left[tail : tail + 4], right[tail : tail + 4]],
                    axis=0,
                )
            )
    return blocks


def orthogonal_kernel(*refs):
    pieces, (_, out, whole, gram, poly, second) = refs[:MATS], refs[MATS:]
    rows = FF // MATS
    tiles = [slice(start, start + TILE) for start in range(0, FF, TILE)]
    squares = jnp.zeros(pieces[0].shape[1:], jnp.float32)
    for number, piece in enumerate(pieces):
        value = piece[...].astype(jnp.float32)
        squares += jnp.sum(value * value, axis=0)
        left, right = unpacked(value)
        place = slice(number * rows, (number + 1) * rows)
        whole[place, :HALF] = left.astype(jnp.bfloat16)
        whole[place, HALF:] = right.astype(jnp.bfloat16)
    norm_square = jnp.full((1, 1), jnp.sum(squares), jnp.float32)
    inverse = 1.0 / (jnp.sqrt(norm_square) + NORM_EPS)
    for tile in tiles:
        product = dot_transposed(whole[tile, :], whole[...])
        gram[tile, :] = (product * (inverse * inverse)).astype(jnp.bfloat16)
    for tile in tiles:
        squared = dot_f32(gram[tile, :], gram[...])
        poly[tile, :] = (COEF_B * gram[tile, :].astype(jnp.float32) + COEF_C * squared).astype(
            jnp.bfloat16
        )
    for tile in tiles:
        combined = COEF_A * whole[tile, :].astype(jnp.float32) + dot_f32(poly[tile, :], whole[...])
        second[tile, :] = (inverse * combined).astype(jnp.bfloat16)
    for tile in tiles:
        gram[tile, :] = dot_transposed(second[tile, :], second[...]).astype(jnp.bfloat16)
    own = gram[:rows, :]
    own_poly = (COEF_B * own.astype(jnp.float32) + COEF_C * dot_f32(own, gram[...])).astype(
        jnp.bfloat16
    )
    combined = COEF_A * second[:rows, :].astype(jnp.float32) + dot_f32(own_poly, second[...])
    scaled = 0.2 * math.sqrt(max(FF, D)) * combined
    for number, block in enumerate(packed_blocks(scaled[:, :HALF], scaled[:, HALF:])):
        out[number] = block.astype(jnp.bfloat16)


def spread_kernel(arrived, out):
    value = arrived[...].astype(jnp.float32)
    left = jnp.concatenate([value[:, :8], value[:, 16:20]], axis=1)
    right = jnp.concatenate([value[:, 8:16], value[:, 20:]], axis=1)
    out[:, :, :HALF] = jnp.swapaxes(left, 0, 1).astype(jnp.bfloat16)
    out[:, :, HALF:] = jnp.swapaxes(right, 0, 1).astype(jnp.bfloat16)


def orthogonal_rows(pieces, stamp):
    return call(
        orthogonal_kernel,
        jax.ShapeDtypeStruct(pieces[0].shape, jnp.bfloat16),
        *pieces,
        stamp,
        scratch=[
            pltpu.VMEM((FF, D), jnp.bfloat16),
            pltpu.VMEM((FF, FF), jnp.bfloat16),
            pltpu.VMEM((FF, FF), jnp.bfloat16),
            pltpu.VMEM((FF, D), jnp.bfloat16),
        ],
        cost=pl.CostEstimate(
            flops=2 * FF * (3 * FF * D + FF * FF), bytes_accessed=2 * FF * D, transcendentals=0
        ),
    )


def exchanged(value, axes, groups=None):
    return lax.all_to_all(value, axes, split_axis=0, concat_axis=0, tiled=True, axis_index_groups=groups)


def gathered(piece):
    def swapped(value, axis, flip):
        size = lax.axis_size(axis)
        return lax.ppermute(value, axis, [(place, place ^ flip) for place in range(size)])

    side, other_side, far = swapped(piece, "x", 1), swapped(piece, "x", 3), swapped(piece, "x", 2)
    plane = swapped(piece, "z", 1)
    return [
        piece,
        side,
        other_side,
        far,
        swapped(far, "z", 1),
        plane,
        swapped(plane, "x", 3),
        swapped(plane, "x", 1),
    ]


def local(gradient, momentum):
    shape = (gradient.shape[1], MATS, D)
    gradient, momentum = jnp.swapaxes(gradient, 0, 1), jnp.swapaxes(momentum, 0, 1)
    whole = jax.ShapeDtypeStruct(shape, jnp.float32)
    squares, kept, decayed = call(
        start_kernel,
        (jax.ShapeDtypeStruct((32, 1, 128), jnp.float32), whole, whole),
        gradient,
        momentum,
        scratch=[pltpu.SemaphoreType.DMA((2,))],
        space=pl.ANY,
        limit=54272,
    )
    squares = exchanged(squares, ("x", "y", "core"))
    squares = call(add_kernel, jax.ShapeDtypeStruct((16, 1, 128), jnp.float32), squares)
    squares = exchanged(squares, "z")
    outgoing = call(
        blend_kernel, jax.ShapeDtypeStruct((MATS, 24, HALF), jnp.bfloat16), squares, kept, decayed
    )
    piece = exchanged(outgoing, "z", PLANES)
    momentum_next, stamp = call(
        follow_kernel, (whole, jax.ShapeDtypeStruct((1, 128), jnp.float32)), squares, kept, decayed
    )
    returning = orthogonal_rows(gathered(piece), stamp)
    arrived = exchanged(returning, "z", PLANES)
    update = call(spread_kernel, jax.ShapeDtypeStruct(shape, jnp.bfloat16), arrived)
    return (jnp.swapaxes(momentum_next, 0, 1), jnp.swapaxes(update, 0, 1))


def solution(mesh):
    split = Mesh(mesh.devices.reshape(16, 4, 4, 2), ("z", "x", "y", "core"))
    spec = P(("y", "core"), ("z", "x"), None)
    return jax.shard_map(local, mesh=split, in_specs=(spec, spec), out_specs=(spec, spec), check_vma=False)
```

```python
import math

import jax
import jax.numpy as jnp
from jax import lax
from jax.experimental import pallas as pl
from jax.experimental.pallas import tpu as pltpu
from jax.sharding import Mesh, PartitionSpec as P

D = 1024
FF = 768
MATS = 8
HALF = D // 2
TILE = 256
BLOCKS = tuple(tuple(range(start, start + 8)) for start in range(0, 64, 8))
PLANES = ((0, 2, 4, 6, 9, 11, 13, 15), (1, 3, 5, 7, 8, 10, 12, 14))


MOMENTUM_RATE = 0.95
RMS_CAP = 0.5
NORM_EPS = 1e-07
COEF_A = 3.4445
COEF_B = -4.775
COEF_C = 2.0315


def dot_f32(left, right):
    return jnp.dot(left, right, preferred_element_type=jnp.float32)


def dot_transposed(left, right):
    return lax.dot_general(left, right, (((1,), (1,)), ((), ())), preferred_element_type=jnp.float32)


def call(kernel, out_shape, *args, scratch=(), cost=None, space=pltpu.VMEM, limit=32768):
    return pl.pallas_call(
        kernel,
        out_shape=out_shape,
        in_specs=[pl.BlockSpec(memory_space=space)] * len(args),
        out_specs=jax.tree.map(lambda _: pl.BlockSpec(memory_space=pltpu.VMEM), out_shape),
        scratch_shapes=scratch,
        compiler_params=pltpu.CompilerParams(vmem_limit_bytes=limit * 1024),
        cost_estimate=cost,
    )(*args)


def start_kernel(gradient, momentum, sums, kept, decayed, arrivals):
    copies = [
        pltpu.make_async_copy(gradient, kept, arrivals.at[0]),
        pltpu.make_async_copy(momentum, decayed, arrivals.at[1]),
    ]
    for copy in copies:
        copy.start()
    copies[0].wait()
    value = kept[...]
    sums[...] = jnp.broadcast_to(jnp.sum(value * value), sums.shape)
    copies[1].wait()
    decayed[...] = MOMENTUM_RATE * decayed[...]


def add_kernel(parts, out):
    out[...] = jnp.broadcast_to(jnp.sum(parts[...], axis=0, keepdims=True), out.shape)


def factor_of(total):
    total_square = jnp.sum(total[...], axis=0)[:, :1]
    factor = jnp.minimum(1.0, RMS_CAP * math.sqrt(MATS * MATS * FF * D) / jnp.sqrt(total_square))
    return factor[None]


def follow_kernel(total, gradient, decayed, momentum_next, stamp):
    momentum_next[...] = decayed[...] + factor_of(total) * gradient[...]
    stamp[...] = jnp.sum(total[...], axis=0)


def blend_kernel(total, gradient, decayed, outgoing):
    scaled = factor_of(total) * gradient[...]
    blended = jnp.swapaxes(scaled + MOMENTUM_RATE * (decayed[...] + scaled), 0, 1)
    left, right = blended[:, :, :HALF], blended[:, :, HALF:]
    packed = jnp.concatenate([left[:, :8], right[:, :8], left[:, 8:], right[:, 8:]], axis=1)
    outgoing[...] = packed.astype(jnp.bfloat16)


def unpacked(value):
    left, right = [], []
    for number in range(0, MATS, 2):
        first, second = value[number], value[number + 1]
        left += [first[:8], second[:8], first[16:20], second[16:20]]
        right += [first[8:16], second[8:16], first[20:], second[20:]]
    return jnp.concatenate(left, axis=0), jnp.concatenate(right, axis=0)


def packed_blocks(left, right):
    blocks = []
    for start in range(0, left.shape[0], 24):
        for place in range(2):
            head, tail = start + 8 * place, start + 16 + 4 * place
            blocks.append(
                jnp.concatenate(
                    [left[head : head + 8], right[head : head + 8], left[tail : tail + 4], right[tail : tail + 4]],
                    axis=0,
                )
            )
    return blocks


def orthogonal_kernel(*refs):
    pieces, _, out, whole, gram, poly, second = refs
    rows = FF // MATS
    tiles = [slice(start, start + TILE) for start in range(0, FF, TILE)]
    squares = jnp.zeros(pieces.shape[2:], jnp.float32)
    for number in range(MATS):
        value = pieces[number].astype(jnp.float32)
        squares += jnp.sum(value * value, axis=0)
        left, right = unpacked(value)
        place = slice(number * rows, (number + 1) * rows)
        whole[place, :HALF] = left.astype(jnp.bfloat16)
        whole[place, HALF:] = right.astype(jnp.bfloat16)
    norm_square = jnp.full((1, 1), jnp.sum(squares), jnp.float32)
    inverse = 1.0 / (jnp.sqrt(norm_square) + NORM_EPS)
    for tile in tiles:
        product = dot_transposed(whole[tile, :], whole[...])
        gram[tile, :] = (product * (inverse * inverse)).astype(jnp.bfloat16)
    for tile in tiles:
        squared = dot_f32(gram[tile, :], gram[...])
        poly[tile, :] = (COEF_B * gram[tile, :].astype(jnp.float32) + COEF_C * squared).astype(
            jnp.bfloat16
        )
    for tile in tiles:
        combined = COEF_A * whole[tile, :].astype(jnp.float32) + dot_f32(poly[tile, :], whole[...])
        second[tile, :] = (inverse * combined).astype(jnp.bfloat16)
    for tile in tiles:
        gram[tile, :] = dot_transposed(second[tile, :], second[...]).astype(jnp.bfloat16)
    member = lax.rem(lax.axis_index("z"), 2) * 4 + lax.axis_index("x")
    place = pl.ds(pl.multiple_of(member * rows, 32), rows)
    own = gram[place, :]
    own_poly = (COEF_B * own.astype(jnp.float32) + COEF_C * dot_f32(own, gram[...])).astype(
        jnp.bfloat16
    )
    combined = COEF_A * second[place, :].astype(jnp.float32) + dot_f32(own_poly, second[...])
    scaled = 0.2 * math.sqrt(max(FF, D)) * combined
    for number, block in enumerate(packed_blocks(scaled[:, :HALF], scaled[:, HALF:])):
        out[number] = block.astype(jnp.bfloat16)


def spread_kernel(arrived, out):
    value = arrived[...].astype(jnp.float32)
    left = jnp.concatenate([value[:, :8], value[:, 16:20]], axis=1)
    right = jnp.concatenate([value[:, 8:16], value[:, 20:]], axis=1)
    out[:, :, :HALF] = jnp.swapaxes(left, 0, 1).astype(jnp.bfloat16)
    out[:, :, HALF:] = jnp.swapaxes(right, 0, 1).astype(jnp.bfloat16)


def orthogonal_rows(pieces, stamp):
    return call(
        orthogonal_kernel,
        jax.ShapeDtypeStruct(pieces.shape[1:], jnp.bfloat16),
        pieces,
        stamp,
        scratch=[
            pltpu.VMEM((FF, D), jnp.bfloat16),
            pltpu.VMEM((FF, FF), jnp.bfloat16),
            pltpu.VMEM((FF, FF), jnp.bfloat16),
            pltpu.VMEM((FF, D), jnp.bfloat16),
        ],
        cost=pl.CostEstimate(
            flops=2 * FF * (3 * FF * D + FF * FF), bytes_accessed=2 * FF * D, transcendentals=0
        ),
    )


def exchanged(value, axes, groups=None):
    return lax.all_to_all(value, axes, split_axis=0, concat_axis=0, tiled=True, axis_index_groups=groups)


def gathered(piece):
    return exchanged(jnp.broadcast_to(piece[None], (MATS, *piece.shape)), ("z", "x"), BLOCKS)


def local(gradient, momentum):
    shape = (gradient.shape[1], MATS, D)
    gradient, momentum = jnp.swapaxes(gradient, 0, 1), jnp.swapaxes(momentum, 0, 1)
    whole = jax.ShapeDtypeStruct(shape, jnp.float32)
    squares, kept, decayed = call(
        start_kernel,
        (jax.ShapeDtypeStruct((32, 1, 128), jnp.float32), whole, whole),
        gradient,
        momentum,
        scratch=[pltpu.SemaphoreType.DMA((2,))],
        space=pl.ANY,
        limit=54272,
    )
    squares = exchanged(squares, ("x", "y", "core"))
    squares = call(add_kernel, jax.ShapeDtypeStruct((16, 1, 128), jnp.float32), squares)
    squares = exchanged(squares, "z")
    outgoing = call(
        blend_kernel, jax.ShapeDtypeStruct((MATS, 24, HALF), jnp.bfloat16), squares, kept, decayed
    )
    piece = exchanged(outgoing, "z", PLANES)
    momentum_next, stamp = call(
        follow_kernel, (whole, jax.ShapeDtypeStruct((1, 128), jnp.float32)), squares, kept, decayed
    )
    returning = orthogonal_rows(gathered(piece), stamp)
    arrived = exchanged(returning, "z", PLANES)
    update = call(spread_kernel, jax.ShapeDtypeStruct(shape, jnp.bfloat16), arrived)
    return (jnp.swapaxes(momentum_next, 0, 1), jnp.swapaxes(update, 0, 1))


def solution(mesh):
    split = Mesh(mesh.devices.reshape(16, 4, 4, 2), ("z", "x", "y", "core"))
    spec = P(("y", "core"), ("z", "x"), None)
    return jax.shard_map(local, mesh=split, in_specs=(spec, spec), out_specs=(spec, spec), check_vma=False)
```

```python
import math

import jax
import jax.numpy as jnp
from jax import lax
from jax.experimental import pallas as pl
from jax.experimental.pallas import tpu as pltpu
from jax.sharding import Mesh, PartitionSpec as P

D = 1024
FF = 768
MATS = 8
HALF = D // 2
TILE = 256
BLOCKS = tuple(tuple(range(start, start + 8)) for start in range(0, 64, 8))
PLANES = ((0, 2, 4, 6, 9, 11, 13, 15), (1, 3, 5, 7, 8, 10, 12, 14))


MOMENTUM_RATE = 0.95
RMS_CAP = 0.5
NORM_EPS = 1e-07
COEF_A = 3.4445
COEF_B = -4.775
COEF_C = 2.0315


def dot_f32(left, right):
    return jnp.dot(left, right, preferred_element_type=jnp.float32)


def dot_transposed(left, right):
    return lax.dot_general(left, right, (((1,), (1,)), ((), ())), preferred_element_type=jnp.float32)


def call(kernel, out_shape, *args, scratch=(), cost=None, space=pltpu.VMEM, limit=32768):
    return pl.pallas_call(
        kernel,
        out_shape=out_shape,
        in_specs=[pl.BlockSpec(memory_space=space)] * len(args),
        out_specs=jax.tree.map(lambda _: pl.BlockSpec(memory_space=pltpu.VMEM), out_shape),
        scratch_shapes=scratch,
        compiler_params=pltpu.CompilerParams(vmem_limit_bytes=limit * 1024),
        cost_estimate=cost,
    )(*args)


def start_kernel(gradient, momentum, sums, kept, decayed, arrivals):
    copies = [
        pltpu.make_async_copy(gradient, kept, arrivals.at[0]),
        pltpu.make_async_copy(momentum, decayed, arrivals.at[1]),
    ]
    for copy in copies:
        copy.start()
    copies[0].wait()
    value = kept[...]
    sums[...] = jnp.broadcast_to(jnp.sum(value * value), sums.shape)
    copies[1].wait()
    decayed[...] = MOMENTUM_RATE * decayed[...]


def add_kernel(parts, out):
    out[...] = jnp.broadcast_to(jnp.sum(parts[...], axis=0, keepdims=True), out.shape)


def factor_of(total):
    total_square = jnp.sum(total[...], axis=0)[:, :1]
    factor = jnp.minimum(1.0, RMS_CAP * math.sqrt(MATS * MATS * FF * D) / jnp.sqrt(total_square))
    return factor[None]


def follow_kernel(total, gradient, decayed, momentum_next, stamp):
    momentum_next[...] = decayed[...] + factor_of(total) * gradient[...]
    stamp[...] = jnp.sum(total[...], axis=0)


def blend_kernel(total, gradient, decayed, outgoing):
    scaled = factor_of(total) * gradient[...]
    blended = jnp.swapaxes(scaled + MOMENTUM_RATE * (decayed[...] + scaled), 0, 1)
    left, right = blended[:, :, :HALF], blended[:, :, HALF:]
    packed = jnp.concatenate([left[:, :8], right[:, :8], left[:, 8:], right[:, 8:]], axis=1)
    outgoing[...] = packed.astype(jnp.bfloat16)


def copy_kernel(piece, out):
    out[...] = jnp.broadcast_to(piece[...][None], out.shape)


def unpacked(value):
    left, right = [], []
    for number in range(0, MATS, 2):
        first, second = value[number], value[number + 1]
        left += [first[:8], second[:8], first[16:20], second[16:20]]
        right += [first[8:16], second[8:16], first[20:], second[20:]]
    return jnp.concatenate(left, axis=0), jnp.concatenate(right, axis=0)


def packed_blocks(left, right):
    blocks = []
    for start in range(0, left.shape[0], 24):
        for place in range(2):
            head, tail = start + 8 * place, start + 16 + 4 * place
            blocks.append(
                jnp.concatenate(
                    [left[head : head + 8], right[head : head + 8], left[tail : tail + 4], right[tail : tail + 4]],
                    axis=0,
                )
            )
    return blocks


def orthogonal_kernel(*refs):
    pieces, _, out, whole, gram, poly, second = refs
    rows = FF // MATS
    tiles = [slice(start, start + TILE) for start in range(0, FF, TILE)]
    squares = jnp.zeros(pieces.shape[2:], jnp.float32)
    member = lax.rem(lax.axis_index("z"), 2) * 4 + lax.axis_index("x")

    def place(source, start):
        value = pieces[source].astype(jnp.float32)
        left, right = unpacked(value)
        whole[pl.ds(start, rows), :HALF] = left.astype(jnp.bfloat16)
        whole[pl.ds(start, rows), HALF:] = right.astype(jnp.bfloat16)
        return jnp.sum(value * value, axis=0)

    for number in range(1, MATS):
        squares += place(number, number * rows)
    squares += place(0, pl.multiple_of(member * rows, 32))
    place(member, 0)
    norm_square = jnp.full((1, 1), jnp.sum(squares), jnp.float32)
    inverse = 1.0 / (jnp.sqrt(norm_square) + NORM_EPS)
    for tile in tiles:
        product = dot_transposed(whole[tile, :], whole[...])
        gram[tile, :] = (product * (inverse * inverse)).astype(jnp.bfloat16)
    for tile in tiles:
        squared = dot_f32(gram[tile, :], gram[...])
        poly[tile, :] = (COEF_B * gram[tile, :].astype(jnp.float32) + COEF_C * squared).astype(
            jnp.bfloat16
        )
    for tile in tiles:
        combined = COEF_A * whole[tile, :].astype(jnp.float32) + dot_f32(poly[tile, :], whole[...])
        second[tile, :] = (inverse * combined).astype(jnp.bfloat16)
    for tile in tiles:
        gram[tile, :] = dot_transposed(second[tile, :], second[...]).astype(jnp.bfloat16)
    own = gram[:rows, :]
    own_poly = (COEF_B * own.astype(jnp.float32) + COEF_C * dot_f32(own, gram[...])).astype(
        jnp.bfloat16
    )
    combined = COEF_A * second[:rows, :].astype(jnp.float32) + dot_f32(own_poly, second[...])
    scaled = 0.2 * math.sqrt(max(FF, D)) * combined
    for number, block in enumerate(packed_blocks(scaled[:, :HALF], scaled[:, HALF:])):
        out[number] = block.astype(jnp.bfloat16)


def spread_kernel(arrived, out):
    value = arrived[...].astype(jnp.float32)
    left = jnp.concatenate([value[:, :8], value[:, 16:20]], axis=1)
    right = jnp.concatenate([value[:, 8:16], value[:, 20:]], axis=1)
    out[:, :, :HALF] = jnp.swapaxes(left, 0, 1).astype(jnp.bfloat16)
    out[:, :, HALF:] = jnp.swapaxes(right, 0, 1).astype(jnp.bfloat16)


def orthogonal_rows(pieces, stamp):
    return call(
        orthogonal_kernel,
        jax.ShapeDtypeStruct(pieces.shape[1:], jnp.bfloat16),
        pieces,
        stamp,
        scratch=[
            pltpu.VMEM((FF, D), jnp.bfloat16),
            pltpu.VMEM((FF, FF), jnp.bfloat16),
            pltpu.VMEM((FF, FF), jnp.bfloat16),
            pltpu.VMEM((FF, D), jnp.bfloat16),
        ],
        cost=pl.CostEstimate(
            flops=2 * FF * (3 * FF * D + FF * FF), bytes_accessed=2 * FF * D, transcendentals=0
        ),
    )


def exchanged(value, axes, groups=None):
    return lax.all_to_all(value, axes, split_axis=0, concat_axis=0, tiled=True, axis_index_groups=groups)


def gathered(piece):
    copies = call(copy_kernel, jax.ShapeDtypeStruct((MATS, *piece.shape), piece.dtype), piece)
    return exchanged(copies, ("z", "x"), BLOCKS)


def local(gradient, momentum):
    shape = (gradient.shape[1], MATS, D)
    gradient, momentum = jnp.swapaxes(gradient, 0, 1), jnp.swapaxes(momentum, 0, 1)
    whole = jax.ShapeDtypeStruct(shape, jnp.float32)
    squares, kept, decayed = call(
        start_kernel,
        (jax.ShapeDtypeStruct((32, 1, 128), jnp.float32), whole, whole),
        gradient,
        momentum,
        scratch=[pltpu.SemaphoreType.DMA((2,))],
        space=pl.ANY,
        limit=54272,
    )
    squares = exchanged(squares, ("x", "y", "core"))
    squares = call(add_kernel, jax.ShapeDtypeStruct((16, 1, 128), jnp.float32), squares)
    squares = exchanged(squares, "z")
    outgoing = call(
        blend_kernel, jax.ShapeDtypeStruct((MATS, 24, HALF), jnp.bfloat16), squares, kept, decayed
    )
    piece = exchanged(outgoing, "z", PLANES)
    momentum_next, stamp = call(
        follow_kernel, (whole, jax.ShapeDtypeStruct((1, 128), jnp.float32)), squares, kept, decayed
    )
    returning = orthogonal_rows(gathered(piece), stamp)
    arrived = exchanged(returning, "z", PLANES)
    update = call(spread_kernel, jax.ShapeDtypeStruct(shape, jnp.bfloat16), arrived)
    return (jnp.swapaxes(momentum_next, 0, 1), jnp.swapaxes(update, 0, 1))


def solution(mesh):
    split = Mesh(mesh.devices.reshape(16, 4, 4, 2), ("z", "x", "y", "core"))
    spec = P(("y", "core"), ("z", "x"), None)
    return jax.shard_map(local, mesh=split, in_specs=(spec, spec), out_specs=(spec, spec), check_vma=False)
```

```python
import math

import jax
import jax.numpy as jnp
from jax import lax
from jax.experimental import pallas as pl
from jax.experimental.pallas import tpu as pltpu
from jax.sharding import Mesh, PartitionSpec as P

D = 1024
FF = 768
MATS = 8
HALF = D // 2
TILE = 256
BLOCKS = tuple(tuple(range(start, start + 8)) for start in range(0, 64, 8))
PLANES = ((0, 2, 4, 6, 9, 11, 13, 15), (1, 3, 5, 7, 8, 10, 12, 14))


MOMENTUM_RATE = 0.95
RMS_CAP = 0.5
NORM_EPS = 1e-07
COEF_A = 3.4445
COEF_B = -4.775
COEF_C = 2.0315


def dot_f32(left, right):
    return jnp.dot(left, right, preferred_element_type=jnp.float32)


def dot_transposed(left, right):
    return lax.dot_general(left, right, (((1,), (1,)), ((), ())), preferred_element_type=jnp.float32)


def call(kernel, out_shape, *args, scratch=(), cost=None, space=pltpu.VMEM, limit=32768):
    return pl.pallas_call(
        kernel,
        out_shape=out_shape,
        in_specs=[pl.BlockSpec(memory_space=space)] * len(args),
        out_specs=jax.tree.map(lambda _: pl.BlockSpec(memory_space=pltpu.VMEM), out_shape),
        scratch_shapes=scratch,
        compiler_params=pltpu.CompilerParams(vmem_limit_bytes=limit * 1024),
        cost_estimate=cost,
    )(*args)


def start_kernel(gradient, momentum, sums, kept, decayed, arrivals):
    copies = [
        pltpu.make_async_copy(gradient, kept, arrivals.at[0]),
        pltpu.make_async_copy(momentum, decayed, arrivals.at[1]),
    ]
    for copy in copies:
        copy.start()
    copies[0].wait()
    value = kept[...]
    sums[...] = jnp.broadcast_to(jnp.sum(value * value), sums.shape)
    copies[1].wait()
    decayed[...] = MOMENTUM_RATE * decayed[...]


def add_kernel(parts, out):
    out[...] = jnp.broadcast_to(jnp.sum(parts[...], axis=0, keepdims=True), out.shape)


def factor_of(total):
    total_square = jnp.sum(total[...], axis=0)[:, :1]
    factor = jnp.minimum(1.0, RMS_CAP * math.sqrt(MATS * MATS * FF * D) / jnp.sqrt(total_square))
    return factor[None]


def blend_kernel(total, gradient, decayed, outgoing):
    scaled = factor_of(total) * gradient[...]
    blended = jnp.swapaxes(scaled + MOMENTUM_RATE * (decayed[...] + scaled), 0, 1)
    left, right = blended[:, :, :HALF], blended[:, :, HALF:]
    packed = jnp.concatenate([left[:, :8], right[:, :8], left[:, 8:], right[:, 8:]], axis=1)
    outgoing[...] = packed.astype(jnp.bfloat16)


def copy_kernel(piece, out):
    out[...] = jnp.broadcast_to(piece[...][None], out.shape)


def unpacked(value):
    left, right = [], []
    for number in range(0, MATS, 2):
        first, second = value[number], value[number + 1]
        left += [first[:8], second[:8], first[16:20], second[16:20]]
        right += [first[8:16], second[8:16], first[20:], second[20:]]
    return jnp.concatenate(left, axis=0), jnp.concatenate(right, axis=0)


def packed_blocks(left, right):
    blocks = []
    for start in range(0, left.shape[0], 24):
        for place in range(2):
            head, tail = start + 8 * place, start + 16 + 4 * place
            blocks.append(
                jnp.concatenate(
                    [left[head : head + 8], right[head : head + 8], left[tail : tail + 4], right[tail : tail + 4]],
                    axis=0,
                )
            )
    return blocks


def orthogonal_kernel(*refs):
    pieces, out, whole, gram, poly, second = refs
    rows = FF // MATS
    tiles = [slice(start, start + TILE) for start in range(0, FF, TILE)]
    squares = jnp.zeros(pieces.shape[2:], jnp.float32)
    member = lax.rem(lax.axis_index("z"), 2) * 4 + lax.axis_index("x")

    def place(source, start):
        value = pieces[source].astype(jnp.float32)
        left, right = unpacked(value)
        whole[pl.ds(start, rows), :HALF] = left.astype(jnp.bfloat16)
        whole[pl.ds(start, rows), HALF:] = right.astype(jnp.bfloat16)
        return jnp.sum(value * value, axis=0)

    for number in range(1, MATS):
        squares += place(number, number * rows)
    squares += place(0, pl.multiple_of(member * rows, 32))
    place(member, 0)
    norm_square = jnp.full((1, 1), jnp.sum(squares), jnp.float32)
    inverse = 1.0 / (jnp.sqrt(norm_square) + NORM_EPS)
    for tile in tiles:
        product = dot_transposed(whole[tile, :], whole[...])
        gram[tile, :] = (product * (inverse * inverse)).astype(jnp.bfloat16)
    for tile in tiles:
        squared = dot_f32(gram[tile, :], gram[...])
        poly[tile, :] = (COEF_B * gram[tile, :].astype(jnp.float32) + COEF_C * squared).astype(
            jnp.bfloat16
        )
    for tile in tiles:
        combined = COEF_A * whole[tile, :].astype(jnp.float32) + dot_f32(poly[tile, :], whole[...])
        second[tile, :] = (inverse * combined).astype(jnp.bfloat16)
    for tile in tiles:
        gram[tile, :] = dot_transposed(second[tile, :], second[...]).astype(jnp.bfloat16)
    own = gram[:rows, :]
    own_poly = (COEF_B * own.astype(jnp.float32) + COEF_C * dot_f32(own, gram[...])).astype(
        jnp.bfloat16
    )
    combined = COEF_A * second[:rows, :].astype(jnp.float32) + dot_f32(own_poly, second[...])
    scaled = 0.2 * math.sqrt(max(FF, D)) * combined
    for number, block in enumerate(packed_blocks(scaled[:, :HALF], scaled[:, HALF:])):
        out[number] = block.astype(jnp.bfloat16)


def finish_kernel(total, gradient, decayed, arrived, momentum_next, out):
    momentum_next[...] = decayed[...] + factor_of(total) * gradient[...]
    value = arrived[...].astype(jnp.float32)
    left = jnp.concatenate([value[:, :8], value[:, 16:20]], axis=1)
    right = jnp.concatenate([value[:, 8:16], value[:, 20:]], axis=1)
    out[:, :, :HALF] = jnp.swapaxes(left, 0, 1).astype(jnp.bfloat16)
    out[:, :, HALF:] = jnp.swapaxes(right, 0, 1).astype(jnp.bfloat16)


def orthogonal_rows(pieces):
    return call(
        orthogonal_kernel,
        jax.ShapeDtypeStruct(pieces.shape[1:], jnp.bfloat16),
        pieces,
        scratch=[
            pltpu.VMEM((FF, D), jnp.bfloat16),
            pltpu.VMEM((FF, FF), jnp.bfloat16),
            pltpu.VMEM((FF, FF), jnp.bfloat16),
            pltpu.VMEM((FF, D), jnp.bfloat16),
        ],
        cost=pl.CostEstimate(
            flops=2 * FF * (3 * FF * D + FF * FF), bytes_accessed=2 * FF * D, transcendentals=0
        ),
    )


def exchanged(value, axes, groups=None):
    return lax.all_to_all(value, axes, split_axis=0, concat_axis=0, tiled=True, axis_index_groups=groups)


def gathered(piece):
    copies = call(copy_kernel, jax.ShapeDtypeStruct((MATS, *piece.shape), piece.dtype), piece)
    return exchanged(copies, ("z", "x"), BLOCKS)


def local(gradient, momentum):
    shape = (gradient.shape[1], MATS, D)
    gradient, momentum = jnp.swapaxes(gradient, 0, 1), jnp.swapaxes(momentum, 0, 1)
    whole = jax.ShapeDtypeStruct(shape, jnp.float32)
    squares, kept, decayed = call(
        start_kernel,
        (jax.ShapeDtypeStruct((32, 1, 128), jnp.float32), whole, whole),
        gradient,
        momentum,
        scratch=[pltpu.SemaphoreType.DMA((2,))],
        space=pl.ANY,
        limit=54272,
    )
    squares = exchanged(squares, ("x", "y", "core"))
    squares = call(add_kernel, jax.ShapeDtypeStruct((16, 1, 128), jnp.float32), squares)
    squares = exchanged(squares, "z")
    outgoing = call(
        blend_kernel, jax.ShapeDtypeStruct((MATS, 24, HALF), jnp.bfloat16), squares, kept, decayed
    )
    piece = exchanged(outgoing, "z", PLANES)
    returning = orthogonal_rows(gathered(piece))
    arrived = exchanged(returning, "z", PLANES)
    momentum_next, update = call(
        finish_kernel,
        (whole, jax.ShapeDtypeStruct(shape, jnp.bfloat16)),
        squares,
        kept,
        decayed,
        arrived,
    )
    return (jnp.swapaxes(momentum_next, 0, 1), jnp.swapaxes(update, 0, 1))


def solution(mesh):
    split = Mesh(mesh.devices.reshape(16, 4, 4, 2), ("z", "x", "y", "core"))
    spec = P(("y", "core"), ("z", "x"), None)
    return jax.shard_map(local, mesh=split, in_specs=(spec, spec), out_specs=(spec, spec), check_vma=False)
```

```python
import math

import jax
import jax.numpy as jnp
from jax import lax
from jax.experimental import pallas as pl
from jax.experimental.pallas import tpu as pltpu
from jax.sharding import Mesh, PartitionSpec as P

D = 1024
FF = 768
MATS = 8
HALF = D // 2
TILE = 256
BLOCKS = tuple(tuple(range(start, start + 8)) for start in range(0, 64, 8))
PLANES = ((0, 2, 4, 6, 9, 11, 13, 15), (1, 3, 5, 7, 8, 10, 12, 14))


MOMENTUM_RATE = 0.95
RMS_CAP = 0.5
NORM_EPS = 1e-07
COEF_A = 3.4445
COEF_B = -4.775
COEF_C = 2.0315


def dot_f32(left, right):
    return jnp.dot(left, right, preferred_element_type=jnp.float32)


def dot_transposed(left, right):
    return lax.dot_general(left, right, (((1,), (1,)), ((), ())), preferred_element_type=jnp.float32)


def call(kernel, out_shape, *args, scratch=(), cost=None, space=pltpu.VMEM, limit=32768):
    return pl.pallas_call(
        kernel,
        out_shape=out_shape,
        in_specs=[pl.BlockSpec(memory_space=space)] * len(args),
        out_specs=jax.tree.map(lambda _: pl.BlockSpec(memory_space=pltpu.VMEM), out_shape),
        scratch_shapes=scratch,
        compiler_params=pltpu.CompilerParams(vmem_limit_bytes=limit * 1024),
        cost_estimate=cost,
    )(*args)


def start_kernel(gradient, momentum, sums, kept, decayed, arrivals):
    copies = [
        pltpu.make_async_copy(gradient, kept, arrivals.at[0]),
        pltpu.make_async_copy(momentum, decayed, arrivals.at[1]),
    ]
    for copy in copies:
        copy.start()
    copies[0].wait()
    value = kept[...]
    sums[...] = jnp.broadcast_to(jnp.sum(value * value), sums.shape)
    copies[1].wait()
    decayed[...] = MOMENTUM_RATE * decayed[...]


def add_kernel(parts, out):
    out[...] = jnp.broadcast_to(jnp.sum(parts[...], axis=0, keepdims=True), out.shape)


def factor_of(total):
    total_square = jnp.sum(total[...], axis=0)[:, :1]
    factor = jnp.minimum(1.0, RMS_CAP * math.sqrt(MATS * MATS * FF * D) / jnp.sqrt(total_square))
    return factor[None]


def blend_kernel(total, gradient, decayed, outgoing):
    scaled = factor_of(total) * gradient[...]
    blended = jnp.swapaxes(scaled + MOMENTUM_RATE * (decayed[...] + scaled), 0, 1)
    left, right = blended[:, :, :HALF], blended[:, :, HALF:]
    packed = jnp.concatenate([left[:, :8], right[:, :8], left[:, 8:], right[:, 8:]], axis=1)
    outgoing[...] = packed.astype(jnp.bfloat16)


def copy_kernel(piece, out):
    value = piece[...].astype(jnp.float32)
    left, right = [], []
    for number in range(0, MATS, 2):
        first, second = value[number], value[number + 1]
        left += [first[:8], second[:8], first[16:20], second[16:20]]
        right += [first[8:16], second[8:16], first[20:], second[20:]]
    for start, parts in ((0, left), (HALF, right)):
        half = jnp.concatenate(parts, axis=0).astype(jnp.bfloat16)
        for number in range(MATS):
            out[number, :, start : start + HALF] = half


def packed_blocks(left, right):
    blocks = []
    for start in range(0, left.shape[0], 24):
        for place in range(2):
            head, tail = start + 8 * place, start + 16 + 4 * place
            blocks.append(
                jnp.concatenate(
                    [left[head : head + 8], right[head : head + 8], left[tail : tail + 4], right[tail : tail + 4]],
                    axis=0,
                )
            )
    return blocks


def orthogonal_kernel(whole, out, gram, poly, second):
    rows = FF // MATS
    tiles = [slice(start, start + TILE) for start in range(0, FF, TILE)]
    on_diagonal = lax.broadcasted_iota(jnp.int32, (TILE, TILE), 0) == lax.broadcasted_iota(
        jnp.int32, (TILE, TILE), 1
    )
    norm_square = jnp.float32(0.0)
    for tile in tiles:
        product = dot_transposed(whole[tile, :], whole[...])
        norm_square += jnp.sum(jnp.where(on_diagonal, product[:, tile], 0.0))
        gram[tile, :] = product.astype(jnp.bfloat16)
    inverse = 1.0 / (jnp.sqrt(jnp.full((1, 1), norm_square, jnp.float32)) + NORM_EPS)
    scale = inverse * inverse
    for tile in tiles:
        squared = scale * dot_f32(gram[tile, :], gram[...])
        poly[tile, :] = (
            scale * (COEF_B * gram[tile, :].astype(jnp.float32) + COEF_C * squared)
        ).astype(jnp.bfloat16)
    for tile in tiles:
        combined = COEF_A * whole[tile, :].astype(jnp.float32) + dot_f32(poly[tile, :], whole[...])
        second[tile, :] = (inverse * combined).astype(jnp.bfloat16)
    for tile in tiles:
        gram[tile, :] = dot_transposed(second[tile, :], second[...]).astype(jnp.bfloat16)
    member = lax.rem(lax.axis_index("z"), 2) * 4 + lax.axis_index("x")
    place = pl.ds(pl.multiple_of(member * rows, 32), rows)
    own = gram[place, :]
    own_poly = (COEF_B * own.astype(jnp.float32) + COEF_C * dot_f32(own, gram[...])).astype(
        jnp.bfloat16
    )
    combined = COEF_A * second[place, :].astype(jnp.float32) + dot_f32(own_poly, second[...])
    scaled = 0.2 * math.sqrt(max(FF, D)) * combined
    for number, block in enumerate(packed_blocks(scaled[:, :HALF], scaled[:, HALF:])):
        out[number] = block.astype(jnp.bfloat16)


def finish_kernel(total, gradient, decayed, arrived, momentum_next, out):
    momentum_next[...] = decayed[...] + factor_of(total) * gradient[...]
    value = arrived[...].astype(jnp.float32)
    left = jnp.concatenate([value[:, :8], value[:, 16:20]], axis=1)
    right = jnp.concatenate([value[:, 8:16], value[:, 20:]], axis=1)
    out[:, :, :HALF] = jnp.swapaxes(left, 0, 1).astype(jnp.bfloat16)
    out[:, :, HALF:] = jnp.swapaxes(right, 0, 1).astype(jnp.bfloat16)


def orthogonal_rows(whole):
    return call(
        orthogonal_kernel,
        jax.ShapeDtypeStruct((MATS, 24, HALF), jnp.bfloat16),
        whole,
        scratch=[
            pltpu.VMEM((FF, FF), jnp.bfloat16),
            pltpu.VMEM((FF, FF), jnp.bfloat16),
            pltpu.VMEM((FF, D), jnp.bfloat16),
        ],
        cost=pl.CostEstimate(
            flops=2 * FF * (3 * FF * D + FF * FF), bytes_accessed=2 * FF * D, transcendentals=0
        ),
    )


def exchanged(value, axes, groups=None):
    return lax.all_to_all(value, axes, split_axis=0, concat_axis=0, tiled=True, axis_index_groups=groups)


def gathered(piece):
    rows = FF // MATS
    copies = call(copy_kernel, jax.ShapeDtypeStruct((MATS, rows, D), piece.dtype), piece)
    return exchanged(copies, ("z", "x"), BLOCKS).reshape(FF, D)


def local(gradient, momentum):
    shape = (gradient.shape[1], MATS, D)
    gradient, momentum = jnp.swapaxes(gradient, 0, 1), jnp.swapaxes(momentum, 0, 1)
    whole = jax.ShapeDtypeStruct(shape, jnp.float32)
    squares, kept, decayed = call(
        start_kernel,
        (jax.ShapeDtypeStruct((32, 1, 128), jnp.float32), whole, whole),
        gradient,
        momentum,
        scratch=[pltpu.SemaphoreType.DMA((2,))],
        space=pl.ANY,
        limit=54272,
    )
    squares = exchanged(squares, ("x", "y", "core"))
    squares = call(add_kernel, jax.ShapeDtypeStruct((16, 1, 128), jnp.float32), squares)
    squares = exchanged(squares, "z")
    outgoing = call(
        blend_kernel, jax.ShapeDtypeStruct((MATS, 24, HALF), jnp.bfloat16), squares, kept, decayed
    )
    piece = exchanged(outgoing, "z", PLANES)
    returning = orthogonal_rows(gathered(piece))
    arrived = exchanged(returning, "z", PLANES)
    momentum_next, update = call(
        finish_kernel,
        (whole, jax.ShapeDtypeStruct(shape, jnp.bfloat16)),
        squares,
        kept,
        decayed,
        arrived,
    )
    return (jnp.swapaxes(momentum_next, 0, 1), jnp.swapaxes(update, 0, 1))


def solution(mesh):
    split = Mesh(mesh.devices.reshape(16, 4, 4, 2), ("z", "x", "y", "core"))
    spec = P(("y", "core"), ("z", "x"), None)
    return jax.shard_map(local, mesh=split, in_specs=(spec, spec), out_specs=(spec, spec), check_vma=False)
```

```python
import math

import jax
import jax.numpy as jnp
from jax import lax
from jax.experimental import pallas as pl
from jax.experimental.pallas import tpu as pltpu
from jax.sharding import Mesh, PartitionSpec as P

D = 1024
FF = 768
MATS = 8
HALF = D // 2
TILE = 256
BLOCKS = tuple(tuple(range(start, start + 8)) for start in range(0, 64, 8))
PLANES = ((0, 2, 4, 6, 9, 11, 13, 15), (1, 3, 5, 7, 8, 10, 12, 14))


MOMENTUM_RATE = 0.95
RMS_CAP = 0.5
NORM_EPS = 1e-07
COEF_A = 3.4445
COEF_B = -4.775
COEF_C = 2.0315


def dot_f32(left, right):
    return jnp.dot(left, right, preferred_element_type=jnp.float32)


def dot_transposed(left, right):
    return lax.dot_general(left, right, (((1,), (1,)), ((), ())), preferred_element_type=jnp.float32)


def call(kernel, out_shape, *args, scratch=(), cost=None, space=pltpu.VMEM, limit=32768):
    return pl.pallas_call(
        kernel,
        out_shape=out_shape,
        in_specs=[pl.BlockSpec(memory_space=space)] * len(args),
        out_specs=jax.tree.map(lambda _: pl.BlockSpec(memory_space=pltpu.VMEM), out_shape),
        scratch_shapes=scratch,
        compiler_params=pltpu.CompilerParams(vmem_limit_bytes=limit * 1024),
        cost_estimate=cost,
    )(*args)


def start_kernel(gradient, momentum, sums, kept, decayed, arrivals):
    copies = [
        pltpu.make_async_copy(gradient, kept, arrivals.at[0]),
        pltpu.make_async_copy(momentum, decayed, arrivals.at[1]),
    ]
    for copy in copies:
        copy.start()
    copies[0].wait()
    value = kept[...]
    sums[...] = jnp.broadcast_to(jnp.sum(value * value), sums.shape)
    copies[1].wait()
    decayed[...] = MOMENTUM_RATE * decayed[...]


def add_kernel(parts, out):
    out[...] = jnp.broadcast_to(jnp.sum(parts[...], axis=0, keepdims=True), out.shape)


def factor_of(total):
    total_square = jnp.sum(total[...], axis=0)[:, :1]
    factor = jnp.minimum(1.0, RMS_CAP * math.sqrt(MATS * MATS * FF * D) / jnp.sqrt(total_square))
    return factor[None]


def blend_kernel(total, gradient, decayed, outgoing):
    scaled = factor_of(total) * gradient[...]
    blended = jnp.swapaxes(scaled + MOMENTUM_RATE * (decayed[...] + scaled), 0, 1)
    left, right = blended[:, :, :HALF], blended[:, :, HALF:]
    packed = jnp.concatenate([left[:, :8], right[:, :8], left[:, 8:], right[:, 8:]], axis=1)
    outgoing[...] = packed.astype(jnp.bfloat16)


def copy_kernel(piece, out):
    value = piece[...].astype(jnp.float32)
    left, right = [], []
    for number in range(0, MATS, 2):
        first, second = value[number], value[number + 1]
        left += [first[:8], second[:8], first[16:20], second[16:20]]
        right += [first[8:16], second[8:16], first[20:], second[20:]]
    for start, parts in ((0, left), (HALF, right)):
        half = jnp.concatenate(parts, axis=0).astype(jnp.bfloat16)
        for number in range(MATS):
            out[number, :, start : start + HALF] = half


def packed_blocks(left, right):
    blocks = []
    for start in range(0, left.shape[0], 24):
        for place in range(2):
            head, tail = start + 8 * place, start + 16 + 4 * place
            blocks.append(
                jnp.concatenate(
                    [left[head : head + 8], right[head : head + 8], left[tail : tail + 4], right[tail : tail + 4]],
                    axis=0,
                )
            )
    return blocks


def orthogonal_kernel(whole, out, gram, poly, second):
    rows = FF // MATS
    tiles = [slice(0, FF)]
    on_diagonal = lax.broadcasted_iota(jnp.int32, (TILE, TILE), 0) == lax.broadcasted_iota(
        jnp.int32, (TILE, TILE), 1
    )
    norm_square = jnp.float32(0.0)
    for tile in tiles:
        product = dot_transposed(whole[tile, :], whole[...])
        for start in range(0, FF, TILE):
            corner = product[start : start + TILE, start : start + TILE]
            norm_square += jnp.sum(jnp.where(on_diagonal, corner, 0.0))
        gram[tile, :] = product.astype(jnp.bfloat16)
    inverse = 1.0 / (jnp.sqrt(jnp.full((1, 1), norm_square, jnp.float32)) + NORM_EPS)
    scale = inverse * inverse
    for tile in tiles:
        squared = scale * dot_f32(gram[tile, :], gram[...])
        poly[tile, :] = (
            scale * (COEF_B * gram[tile, :].astype(jnp.float32) + COEF_C * squared)
        ).astype(jnp.bfloat16)
    for tile in tiles:
        combined = COEF_A * whole[tile, :].astype(jnp.float32) + dot_f32(poly[tile, :], whole[...])
        second[tile, :] = (inverse * combined).astype(jnp.bfloat16)
    for tile in tiles:
        gram[tile, :] = dot_transposed(second[tile, :], second[...]).astype(jnp.bfloat16)
    member = lax.rem(lax.axis_index("z"), 2) * 4 + lax.axis_index("x")
    place = pl.ds(pl.multiple_of(member * rows, 32), rows)
    own = gram[place, :]
    own_poly = (COEF_B * own.astype(jnp.float32) + COEF_C * dot_f32(own, gram[...])).astype(
        jnp.bfloat16
    )
    combined = COEF_A * second[place, :].astype(jnp.float32) + dot_f32(own_poly, second[...])
    scaled = 0.2 * math.sqrt(max(FF, D)) * combined
    for number, block in enumerate(packed_blocks(scaled[:, :HALF], scaled[:, HALF:])):
        out[number] = block.astype(jnp.bfloat16)


def finish_kernel(total, gradient, decayed, arrived, momentum_next, out):
    momentum_next[...] = decayed[...] + factor_of(total) * gradient[...]
    value = arrived[...].astype(jnp.float32)
    left = jnp.concatenate([value[:, :8], value[:, 16:20]], axis=1)
    right = jnp.concatenate([value[:, 8:16], value[:, 20:]], axis=1)
    out[:, :, :HALF] = jnp.swapaxes(left, 0, 1).astype(jnp.bfloat16)
    out[:, :, HALF:] = jnp.swapaxes(right, 0, 1).astype(jnp.bfloat16)


def orthogonal_rows(whole):
    return call(
        orthogonal_kernel,
        jax.ShapeDtypeStruct((MATS, 24, HALF), jnp.bfloat16),
        whole,
        scratch=[
            pltpu.VMEM((FF, FF), jnp.bfloat16),
            pltpu.VMEM((FF, FF), jnp.bfloat16),
            pltpu.VMEM((FF, D), jnp.bfloat16),
        ],
        cost=pl.CostEstimate(
            flops=2 * FF * (3 * FF * D + FF * FF), bytes_accessed=2 * FF * D, transcendentals=0
        ),
    )


def exchanged(value, axes, groups=None):
    return lax.all_to_all(value, axes, split_axis=0, concat_axis=0, tiled=True, axis_index_groups=groups)


def gathered(piece):
    rows = FF // MATS
    copies = call(copy_kernel, jax.ShapeDtypeStruct((MATS, rows, D), piece.dtype), piece)
    return exchanged(copies, ("z", "x"), BLOCKS).reshape(FF, D)


def local(gradient, momentum):
    shape = (gradient.shape[1], MATS, D)
    gradient, momentum = jnp.swapaxes(gradient, 0, 1), jnp.swapaxes(momentum, 0, 1)
    whole = jax.ShapeDtypeStruct(shape, jnp.float32)
    squares, kept, decayed = call(
        start_kernel,
        (jax.ShapeDtypeStruct((32, 1, 128), jnp.float32), whole, whole),
        gradient,
        momentum,
        scratch=[pltpu.SemaphoreType.DMA((2,))],
        space=pl.ANY,
        limit=54272,
    )
    squares = exchanged(squares, ("x", "y", "core"))
    squares = call(add_kernel, jax.ShapeDtypeStruct((16, 1, 128), jnp.float32), squares)
    squares = exchanged(squares, "z")
    outgoing = call(
        blend_kernel, jax.ShapeDtypeStruct((MATS, 24, HALF), jnp.bfloat16), squares, kept, decayed
    )
    piece = exchanged(outgoing, "z", PLANES)
    returning = orthogonal_rows(gathered(piece))
    arrived = exchanged(returning, "z", PLANES)
    momentum_next, update = call(
        finish_kernel,
        (whole, jax.ShapeDtypeStruct(shape, jnp.bfloat16)),
        squares,
        kept,
        decayed,
        arrived,
    )
    return (jnp.swapaxes(momentum_next, 0, 1), jnp.swapaxes(update, 0, 1))


def solution(mesh):
    split = Mesh(mesh.devices.reshape(16, 4, 4, 2), ("z", "x", "y", "core"))
    spec = P(("y", "core"), ("z", "x"), None)
    return jax.shard_map(local, mesh=split, in_specs=(spec, spec), out_specs=(spec, spec), check_vma=False)
```

```python
import math

import jax
import jax.numpy as jnp
from jax import lax
from jax.experimental import pallas as pl
from jax.experimental.pallas import tpu as pltpu
from jax.sharding import Mesh, PartitionSpec as P

D = 1024
FF = 768
MATS = 8
HALF = D // 2
TILE = 256
BLOCKS = tuple(tuple(range(start, start + 8)) for start in range(0, 64, 8))
PLANES = ((0, 2, 4, 6, 9, 11, 13, 15), (1, 3, 5, 7, 8, 10, 12, 14))


MOMENTUM_RATE = 0.95
RMS_CAP = 0.5
NORM_EPS = 1e-07
COEF_A = 3.4445
COEF_B = -4.775
COEF_C = 2.0315


def dot_f32(left, right):
    return jnp.dot(left, right, preferred_element_type=jnp.float32)


def dot_transposed(left, right):
    return lax.dot_general(left, right, (((1,), (1,)), ((), ())), preferred_element_type=jnp.float32)


def call(kernel, out_shape, *args, scratch=(), cost=None, space=pltpu.VMEM, limit=32768):
    return pl.pallas_call(
        kernel,
        out_shape=out_shape,
        in_specs=[pl.BlockSpec(memory_space=space)] * len(args),
        out_specs=jax.tree.map(lambda _: pl.BlockSpec(memory_space=pltpu.VMEM), out_shape),
        scratch_shapes=scratch,
        compiler_params=pltpu.CompilerParams(vmem_limit_bytes=limit * 1024),
        cost_estimate=cost,
    )(*args)


def start_kernel(gradient, momentum, sums, kept, decayed, arrivals):
    copies = [
        pltpu.make_async_copy(gradient, kept, arrivals.at[0]),
        pltpu.make_async_copy(momentum, decayed, arrivals.at[1]),
    ]
    for copy in copies:
        copy.start()
    copies[0].wait()
    value = kept[...]
    sums[...] = jnp.broadcast_to(jnp.sum(value * value), sums.shape)
    copies[1].wait()
    decayed[...] = MOMENTUM_RATE * decayed[...]


def add_kernel(parts, out):
    out[...] = jnp.broadcast_to(jnp.sum(parts[...], axis=0, keepdims=True), out.shape)


def factor_of(total):
    total_square = jnp.sum(total[...], axis=0)[:, :1]
    factor = jnp.minimum(1.0, RMS_CAP * math.sqrt(MATS * MATS * FF * D) / jnp.sqrt(total_square))
    return factor[None]


def blend_kernel(total, gradient, decayed, outgoing):
    scaled = factor_of(total) * gradient[...]
    blended = jnp.swapaxes(scaled + MOMENTUM_RATE * (decayed[...] + scaled), 0, 1)
    left, right = blended[:, :, :HALF], blended[:, :, HALF:]
    packed = jnp.concatenate([left[:, :8], right[:, :8], left[:, 8:], right[:, 8:]], axis=1)
    outgoing[...] = packed.astype(jnp.bfloat16)


def copy_kernel(piece, out):
    value = piece[...].astype(jnp.float32)
    left, right = [], []
    for number in range(0, MATS, 2):
        first, second = value[number], value[number + 1]
        left += [first[:8], second[:8], first[16:20], second[16:20]]
        right += [first[8:16], second[8:16], first[20:], second[20:]]
    for start, parts in ((0, left), (HALF, right)):
        half = jnp.concatenate(parts, axis=0).astype(jnp.bfloat16)
        for number in range(MATS):
            out[number, :, start : start + HALF] = half


def packed_blocks(left, right):
    blocks = []
    for start in range(0, left.shape[0], 24):
        for place in range(2):
            head, tail = start + 8 * place, start + 16 + 4 * place
            blocks.append(
                jnp.concatenate(
                    [left[head : head + 8], right[head : head + 8], left[tail : tail + 4], right[tail : tail + 4]],
                    axis=0,
                )
            )
    return blocks


def orthogonal_kernel(whole, out, gram, poly, second):
    rows = FF // MATS
    tiles = [slice(start, start + TILE) for start in range(0, FF, TILE)]
    on_diagonal = lax.broadcasted_iota(jnp.int32, (TILE, TILE), 0) == lax.broadcasted_iota(
        jnp.int32, (TILE, TILE), 1
    )
    norm_square = jnp.float32(0.0)
    for tile in tiles:
        product = dot_transposed(whole[...], whole[tile, :])
        norm_square += jnp.sum(jnp.where(on_diagonal, product[tile, :], 0.0))
        gram[:, tile] = product.astype(jnp.bfloat16)
    inverse = 1.0 / (jnp.sqrt(jnp.full((1, 1), norm_square, jnp.float32)) + NORM_EPS)
    scale = inverse * inverse
    for tile in tiles:
        squared = scale * dot_f32(gram[...], gram[:, tile])
        poly[:, tile] = (
            scale * (COEF_B * gram[:, tile].astype(jnp.float32) + COEF_C * squared)
        ).astype(jnp.bfloat16)
    for start in range(0, D, TILE):
        tile = slice(start, start + TILE)
        combined = COEF_A * whole[:, tile].astype(jnp.float32) + dot_f32(poly[...], whole[:, tile])
        second[:, tile] = (inverse * combined).astype(jnp.bfloat16)
    for tile in tiles:
        gram[:, tile] = dot_transposed(second[...], second[tile, :]).astype(jnp.bfloat16)
    member = lax.rem(lax.axis_index("z"), 2) * 4 + lax.axis_index("x")
    place = pl.ds(pl.multiple_of(member * rows, 32), rows)
    own = gram[place, :]
    own_poly = (COEF_B * own.astype(jnp.float32) + COEF_C * dot_f32(own, gram[...])).astype(
        jnp.bfloat16
    )
    combined = COEF_A * second[place, :].astype(jnp.float32) + dot_f32(own_poly, second[...])
    scaled = 0.2 * math.sqrt(max(FF, D)) * combined
    for number, block in enumerate(packed_blocks(scaled[:, :HALF], scaled[:, HALF:])):
        out[number] = block.astype(jnp.bfloat16)


def finish_kernel(total, gradient, decayed, arrived, momentum_next, out):
    momentum_next[...] = decayed[...] + factor_of(total) * gradient[...]
    value = arrived[...].astype(jnp.float32)
    left = jnp.concatenate([value[:, :8], value[:, 16:20]], axis=1)
    right = jnp.concatenate([value[:, 8:16], value[:, 20:]], axis=1)
    out[:, :, :HALF] = jnp.swapaxes(left, 0, 1).astype(jnp.bfloat16)
    out[:, :, HALF:] = jnp.swapaxes(right, 0, 1).astype(jnp.bfloat16)


def orthogonal_rows(whole):
    return call(
        orthogonal_kernel,
        jax.ShapeDtypeStruct((MATS, 24, HALF), jnp.bfloat16),
        whole,
        scratch=[
            pltpu.VMEM((FF, FF), jnp.bfloat16),
            pltpu.VMEM((FF, FF), jnp.bfloat16),
            pltpu.VMEM((FF, D), jnp.bfloat16),
        ],
        cost=pl.CostEstimate(
            flops=2 * FF * (3 * FF * D + FF * FF), bytes_accessed=2 * FF * D, transcendentals=0
        ),
    )


def exchanged(value, axes, groups=None):
    return lax.all_to_all(value, axes, split_axis=0, concat_axis=0, tiled=True, axis_index_groups=groups)


def gathered(piece):
    rows = FF // MATS
    copies = call(copy_kernel, jax.ShapeDtypeStruct((MATS, rows, D), piece.dtype), piece)
    return exchanged(copies, ("z", "x"), BLOCKS).reshape(FF, D)


def local(gradient, momentum):
    shape = (gradient.shape[1], MATS, D)
    gradient, momentum = jnp.swapaxes(gradient, 0, 1), jnp.swapaxes(momentum, 0, 1)
    whole = jax.ShapeDtypeStruct(shape, jnp.float32)
    squares, kept, decayed = call(
        start_kernel,
        (jax.ShapeDtypeStruct((32, 1, 128), jnp.float32), whole, whole),
        gradient,
        momentum,
        scratch=[pltpu.SemaphoreType.DMA((2,))],
        space=pl.ANY,
        limit=54272,
    )
    squares = exchanged(squares, ("x", "y", "core"))
    squares = call(add_kernel, jax.ShapeDtypeStruct((16, 1, 128), jnp.float32), squares)
    squares = exchanged(squares, "z")
    outgoing = call(
        blend_kernel, jax.ShapeDtypeStruct((MATS, 24, HALF), jnp.bfloat16), squares, kept, decayed
    )
    piece = exchanged(outgoing, "z", PLANES)
    returning = orthogonal_rows(gathered(piece))
    arrived = exchanged(returning, "z", PLANES)
    momentum_next, update = call(
        finish_kernel,
        (whole, jax.ShapeDtypeStruct(shape, jnp.bfloat16)),
        squares,
        kept,
        decayed,
        arrived,
    )
    return (jnp.swapaxes(momentum_next, 0, 1), jnp.swapaxes(update, 0, 1))


def solution(mesh):
    split = Mesh(mesh.devices.reshape(16, 4, 4, 2), ("z", "x", "y", "core"))
    spec = P(("y", "core"), ("z", "x"), None)
    return jax.shard_map(local, mesh=split, in_specs=(spec, spec), out_specs=(spec, spec), check_vma=False)
```

```python
import math

import jax
import jax.numpy as jnp
from jax import lax
from jax.experimental import pallas as pl
from jax.experimental.pallas import tpu as pltpu
from jax.sharding import Mesh, PartitionSpec as P

D = 1024
FF = 768
MATS = 8
HALF = D // 2
TILE = 128
BLOCKS = tuple(tuple(range(start, start + 8)) for start in range(0, 64, 8))
PLANES = ((0, 2, 4, 6, 9, 11, 13, 15), (1, 3, 5, 7, 8, 10, 12, 14))


MOMENTUM_RATE = 0.95
RMS_CAP = 0.5
NORM_EPS = 1e-07
COEF_A = 3.4445
COEF_B = -4.775
COEF_C = 2.0315


def dot_f32(left, right):
    return jnp.dot(left, right, preferred_element_type=jnp.float32)


def dot_transposed(left, right):
    return lax.dot_general(left, right, (((1,), (1,)), ((), ())), preferred_element_type=jnp.float32)


def call(kernel, out_shape, *args, scratch=(), cost=None, space=pltpu.VMEM, limit=32768):
    return pl.pallas_call(
        kernel,
        out_shape=out_shape,
        in_specs=[pl.BlockSpec(memory_space=space)] * len(args),
        out_specs=jax.tree.map(lambda _: pl.BlockSpec(memory_space=pltpu.VMEM), out_shape),
        scratch_shapes=scratch,
        compiler_params=pltpu.CompilerParams(vmem_limit_bytes=limit * 1024),
        cost_estimate=cost,
    )(*args)


def start_kernel(gradient, momentum, sums, kept, decayed, arrivals):
    copies = [
        pltpu.make_async_copy(gradient, kept, arrivals.at[0]),
        pltpu.make_async_copy(momentum, decayed, arrivals.at[1]),
    ]
    for copy in copies:
        copy.start()
    copies[0].wait()
    value = kept[...]
    sums[...] = jnp.broadcast_to(jnp.sum(value * value), sums.shape)
    copies[1].wait()
    decayed[...] = MOMENTUM_RATE * decayed[...]


def add_kernel(parts, out):
    out[...] = jnp.broadcast_to(jnp.sum(parts[...], axis=0, keepdims=True), out.shape)


def factor_of(total):
    total_square = jnp.sum(total[...], axis=0)[:, :1]
    factor = jnp.minimum(1.0, RMS_CAP * math.sqrt(MATS * MATS * FF * D) / jnp.sqrt(total_square))
    return factor[None]


def blend_kernel(total, gradient, decayed, outgoing):
    scaled = factor_of(total) * gradient[...]
    blended = jnp.swapaxes(scaled + MOMENTUM_RATE * (decayed[...] + scaled), 0, 1)
    left, right = blended[:, :, :HALF], blended[:, :, HALF:]
    packed = jnp.concatenate([left[:, :8], right[:, :8], left[:, 8:], right[:, 8:]], axis=1)
    outgoing[...] = packed.astype(jnp.bfloat16)


def copy_kernel(piece, out):
    value = piece[...].astype(jnp.float32)
    left, right = [], []
    for number in range(0, MATS, 2):
        first, second = value[number], value[number + 1]
        left += [first[:8], second[:8], first[16:20], second[16:20]]
        right += [first[8:16], second[8:16], first[20:], second[20:]]
    for start, parts in ((0, left), (HALF, right)):
        half = jnp.concatenate(parts, axis=0).astype(jnp.bfloat16)
        for number in range(MATS):
            out[number, :, start : start + HALF] = half


def packed_blocks(left, right):
    blocks = []
    for start in range(0, left.shape[0], 24):
        for place in range(2):
            head, tail = start + 8 * place, start + 16 + 4 * place
            blocks.append(
                jnp.concatenate(
                    [left[head : head + 8], right[head : head + 8], left[tail : tail + 4], right[tail : tail + 4]],
                    axis=0,
                )
            )
    return blocks


def orthogonal_kernel(whole, out, gram, poly, second):
    rows = FF // MATS
    tiles = [slice(start, start + TILE) for start in range(0, FF, TILE)]
    on_diagonal = lax.broadcasted_iota(jnp.int32, (TILE, TILE), 0) == lax.broadcasted_iota(
        jnp.int32, (TILE, TILE), 1
    )
    norm_square = jnp.float32(0.0)
    for tile in tiles:
        product = dot_transposed(whole[tile, :], whole[...])
        norm_square += jnp.sum(jnp.where(on_diagonal, product[:, tile], 0.0))
        gram[tile, :] = product.astype(jnp.bfloat16)
    inverse = 1.0 / (jnp.sqrt(jnp.full((1, 1), norm_square, jnp.float32)) + NORM_EPS)
    scale = inverse * inverse
    for tile in tiles:
        squared = scale * dot_f32(gram[tile, :], gram[...])
        poly[tile, :] = (
            scale * (COEF_B * gram[tile, :].astype(jnp.float32) + COEF_C * squared)
        ).astype(jnp.bfloat16)
    for tile in tiles:
        combined = COEF_A * whole[tile, :].astype(jnp.float32) + dot_f32(poly[tile, :], whole[...])
        second[tile, :] = (inverse * combined).astype(jnp.bfloat16)
    for tile in tiles:
        gram[tile, :] = dot_transposed(second[tile, :], second[...]).astype(jnp.bfloat16)
    member = lax.rem(lax.axis_index("z"), 2) * 4 + lax.axis_index("x")
    place = pl.ds(pl.multiple_of(member * rows, 32), rows)
    own = gram[place, :]
    own_poly = (COEF_B * own.astype(jnp.float32) + COEF_C * dot_f32(own, gram[...])).astype(
        jnp.bfloat16
    )
    combined = COEF_A * second[place, :].astype(jnp.float32) + dot_f32(own_poly, second[...])
    scaled = 0.2 * math.sqrt(max(FF, D)) * combined
    for number, block in enumerate(packed_blocks(scaled[:, :HALF], scaled[:, HALF:])):
        out[number] = block.astype(jnp.bfloat16)


def finish_kernel(total, gradient, decayed, arrived, momentum_next, out):
    momentum_next[...] = decayed[...] + factor_of(total) * gradient[...]
    value = arrived[...].astype(jnp.float32)
    left = jnp.concatenate([value[:, :8], value[:, 16:20]], axis=1)
    right = jnp.concatenate([value[:, 8:16], value[:, 20:]], axis=1)
    out[:, :, :HALF] = jnp.swapaxes(left, 0, 1).astype(jnp.bfloat16)
    out[:, :, HALF:] = jnp.swapaxes(right, 0, 1).astype(jnp.bfloat16)


def orthogonal_rows(whole):
    return call(
        orthogonal_kernel,
        jax.ShapeDtypeStruct((MATS, 24, HALF), jnp.bfloat16),
        whole,
        scratch=[
            pltpu.VMEM((FF, FF), jnp.bfloat16),
            pltpu.VMEM((FF, FF), jnp.bfloat16),
            pltpu.VMEM((FF, D), jnp.bfloat16),
        ],
        cost=pl.CostEstimate(
            flops=2 * FF * (3 * FF * D + FF * FF), bytes_accessed=2 * FF * D, transcendentals=0
        ),
    )


def exchanged(value, axes, groups=None):
    return lax.all_to_all(value, axes, split_axis=0, concat_axis=0, tiled=True, axis_index_groups=groups)


def gathered(piece):
    rows = FF // MATS
    copies = call(copy_kernel, jax.ShapeDtypeStruct((MATS, rows, D), piece.dtype), piece)
    return exchanged(copies, ("z", "x"), BLOCKS).reshape(FF, D)


def local(gradient, momentum):
    shape = (gradient.shape[1], MATS, D)
    gradient, momentum = jnp.swapaxes(gradient, 0, 1), jnp.swapaxes(momentum, 0, 1)
    whole = jax.ShapeDtypeStruct(shape, jnp.float32)
    squares, kept, decayed = call(
        start_kernel,
        (jax.ShapeDtypeStruct((32, 1, 128), jnp.float32), whole, whole),
        gradient,
        momentum,
        scratch=[pltpu.SemaphoreType.DMA((2,))],
        space=pl.ANY,
        limit=54272,
    )
    squares = exchanged(squares, ("x", "y", "core"))
    squares = call(add_kernel, jax.ShapeDtypeStruct((16, 1, 128), jnp.float32), squares)
    squares = exchanged(squares, "z")
    outgoing = call(
        blend_kernel, jax.ShapeDtypeStruct((MATS, 24, HALF), jnp.bfloat16), squares, kept, decayed
    )
    piece = exchanged(outgoing, "z", PLANES)
    returning = orthogonal_rows(gathered(piece))
    arrived = exchanged(returning, "z", PLANES)
    momentum_next, update = call(
        finish_kernel,
        (whole, jax.ShapeDtypeStruct(shape, jnp.bfloat16)),
        squares,
        kept,
        decayed,
        arrived,
    )
    return (jnp.swapaxes(momentum_next, 0, 1), jnp.swapaxes(update, 0, 1))


def solution(mesh):
    split = Mesh(mesh.devices.reshape(16, 4, 4, 2), ("z", "x", "y", "core"))
    spec = P(("y", "core"), ("z", "x"), None)
    return jax.shard_map(local, mesh=split, in_specs=(spec, spec), out_specs=(spec, spec), check_vma=False)
```

```python
import math

import jax
import jax.numpy as jnp
from jax import lax
from jax.experimental import pallas as pl
from jax.experimental.pallas import tpu as pltpu
from jax.sharding import Mesh, PartitionSpec as P

D = 1024
FF = 768
MATS = 8
HALF = D // 2
TILE = 256
BLOCKS = tuple(tuple(range(start, start + 8)) for start in range(0, 64, 8))
PLANES = ((0, 2, 4, 6, 9, 11, 13, 15), (1, 3, 5, 7, 8, 10, 12, 14))


MOMENTUM_RATE = 0.95
RMS_CAP = 0.5
NORM_EPS = 1e-07
COEF_A = 3.4445
COEF_B = -4.775
COEF_C = 2.0315


def dot_f32(left, right):
    return jnp.dot(left, right, preferred_element_type=jnp.float32)


def dot_transposed(left, right):
    return lax.dot_general(left, right, (((1,), (1,)), ((), ())), preferred_element_type=jnp.float32)


def call(kernel, out_shape, *args, scratch=(), cost=None, space=pltpu.VMEM, limit=32768):
    return pl.pallas_call(
        kernel,
        out_shape=out_shape,
        in_specs=[pl.BlockSpec(memory_space=space)] * len(args),
        out_specs=jax.tree.map(lambda _: pl.BlockSpec(memory_space=pltpu.VMEM), out_shape),
        scratch_shapes=scratch,
        compiler_params=pltpu.CompilerParams(vmem_limit_bytes=limit * 1024),
        cost_estimate=cost,
    )(*args)


def start_kernel(gradient, momentum, sums, kept, decayed, arrivals):
    copies = [
        pltpu.make_async_copy(gradient, kept, arrivals.at[0]),
        pltpu.make_async_copy(momentum, decayed, arrivals.at[1]),
    ]
    for copy in copies:
        copy.start()
    copies[0].wait()
    value = kept[...]
    sums[...] = jnp.broadcast_to(jnp.sum(value * value), sums.shape)
    copies[1].wait()
    decayed[...] = MOMENTUM_RATE * decayed[...]


def add_kernel(parts, out):
    out[...] = jnp.broadcast_to(jnp.sum(parts[...], axis=0, keepdims=True), out.shape)


def factor_of(total):
    total_square = jnp.sum(total[...], axis=0)[:, :1]
    factor = jnp.minimum(1.0, RMS_CAP * math.sqrt(MATS * MATS * FF * D) / jnp.sqrt(total_square))
    return factor[None]


def blend_kernel(total, gradient, decayed, outgoing):
    scaled = factor_of(total) * gradient[...]
    blended = jnp.swapaxes(scaled + MOMENTUM_RATE * (decayed[...] + scaled), 0, 1)
    left, right = blended[:, :, :HALF], blended[:, :, HALF:]
    packed = jnp.concatenate([left[:, :8], right[:, :8], left[:, 8:], right[:, 8:]], axis=1)
    outgoing[...] = packed.astype(jnp.bfloat16)


def copy_kernel(piece, out):
    value = piece[...].astype(jnp.float32)
    left, right = [], []
    for number in range(0, MATS, 2):
        first, second = value[number], value[number + 1]
        left += [first[:8], second[:8], first[16:20], second[16:20]]
        right += [first[8:16], second[8:16], first[20:], second[20:]]
    for start, parts in ((0, left), (HALF, right)):
        half = jnp.concatenate(parts, axis=0).astype(jnp.bfloat16)
        for number in range(MATS):
            out[number, :, start : start + HALF] = half


def packed_blocks(left, right):
    blocks = []
    for start in range(0, left.shape[0], 24):
        for place in range(2):
            head, tail = start + 8 * place, start + 16 + 4 * place
            blocks.append(
                jnp.concatenate(
                    [left[head : head + 8], right[head : head + 8], left[tail : tail + 4], right[tail : tail + 4]],
                    axis=0,
                )
            )
    return blocks


def orthogonal_kernel(whole, out, gram, poly, second):
    rows = FF // MATS
    tiles = [slice(start, start + TILE) for start in range(0, FF, TILE)]
    on_diagonal = lax.broadcasted_iota(jnp.int32, (TILE, TILE), 0) == lax.broadcasted_iota(
        jnp.int32, (TILE, TILE), 1
    )
    norm_square = jnp.float32(0.0)
    for tile in tiles:
        product = dot_transposed(whole[tile, :], whole[...])
        norm_square += jnp.sum(jnp.where(on_diagonal, product[:, tile], 0.0))
        gram[tile, :] = product.astype(jnp.bfloat16)
    inverse = 1.0 / (jnp.sqrt(jnp.full((1, 1), norm_square, jnp.float32)) + NORM_EPS)
    scale = inverse * inverse
    for tile in tiles:
        squared = scale * dot_f32(gram[tile, :], gram[...])
        poly[tile, :] = (
            scale * (COEF_B * gram[tile, :].astype(jnp.float32) + COEF_C * squared)
        ).astype(jnp.bfloat16)
    for tile in tiles:
        combined = COEF_A * whole[tile, :].astype(jnp.float32) + dot_f32(poly[tile, :], whole[...])
        second[tile, :] = (inverse * combined).astype(jnp.bfloat16)
    for tile in tiles:
        gram[tile, :] = dot_transposed(second[tile, :], second[...]).astype(jnp.bfloat16)
    member = lax.rem(lax.axis_index("z"), 2) * 4 + lax.axis_index("x")
    place = pl.ds(pl.multiple_of(member * rows, 32), rows)
    own = gram[place, :]
    own_poly = (COEF_B * own.astype(jnp.float32) + COEF_C * dot_f32(own, gram[...])).astype(
        jnp.bfloat16
    )
    combined = COEF_A * second[place, :].astype(jnp.float32) + dot_f32(own_poly, second[...])
    scaled = 0.2 * math.sqrt(max(FF, D)) * combined
    for number, block in enumerate(packed_blocks(scaled[:, :HALF], scaled[:, HALF:])):
        out[number] = block.astype(jnp.bfloat16)


def finish_kernel(total, gradient, decayed, arrived, momentum_next, out):
    momentum_next[...] = decayed[...] + factor_of(total) * gradient[...]
    value = arrived[...].astype(jnp.float32)
    left = jnp.concatenate([value[:, :8], value[:, 16:20]], axis=1)
    right = jnp.concatenate([value[:, 8:16], value[:, 20:]], axis=1)
    out[:, :, :HALF] = jnp.swapaxes(left, 0, 1).astype(jnp.bfloat16)
    out[:, :, HALF:] = jnp.swapaxes(right, 0, 1).astype(jnp.bfloat16)


def orthogonal_rows(whole):
    return call(
        orthogonal_kernel,
        jax.ShapeDtypeStruct((MATS, 24, HALF), jnp.bfloat16),
        whole,
        scratch=[
            pltpu.VMEM((FF, FF), jnp.bfloat16),
            pltpu.VMEM((FF, FF), jnp.bfloat16),
            pltpu.VMEM((FF, D), jnp.bfloat16),
        ],
        cost=pl.CostEstimate(
            flops=2 * FF * (3 * FF * D + FF * FF), bytes_accessed=2 * FF * D, transcendentals=0
        ),
    )


def exchanged(value, axes, groups=None):
    return lax.all_to_all(value, axes, split_axis=0, concat_axis=0, tiled=True, axis_index_groups=groups)


def gathered(piece):
    rows = FF // MATS
    copies = call(copy_kernel, jax.ShapeDtypeStruct((MATS, rows, D), piece.dtype), piece)
    return exchanged(copies, ("z", "x"), BLOCKS).reshape(FF, D)


def local(gradient, momentum):
    shape = (gradient.shape[1], MATS, D)
    gradient, momentum = jnp.swapaxes(gradient, 0, 1), jnp.swapaxes(momentum, 0, 1)
    whole = jax.ShapeDtypeStruct(shape, jnp.float32)
    squares, kept, decayed = call(
        start_kernel,
        (jax.ShapeDtypeStruct((16, 1, 128), jnp.float32), whole, whole),
        gradient,
        momentum,
        scratch=[pltpu.SemaphoreType.DMA((2,))],
        space=pl.ANY,
        limit=54272,
    )
    squares = exchanged(squares, ("x", "y"))
    squares = call(add_kernel, jax.ShapeDtypeStruct((32, 1, 128), jnp.float32), squares)
    squares = exchanged(squares, ("z", "core"))
    outgoing = call(
        blend_kernel, jax.ShapeDtypeStruct((MATS, 24, HALF), jnp.bfloat16), squares, kept, decayed
    )
    piece = exchanged(outgoing, "z", PLANES)
    returning = orthogonal_rows(gathered(piece))
    arrived = exchanged(returning, "z", PLANES)
    momentum_next, update = call(
        finish_kernel,
        (whole, jax.ShapeDtypeStruct(shape, jnp.bfloat16)),
        squares,
        kept,
        decayed,
        arrived,
    )
    return (jnp.swapaxes(momentum_next, 0, 1), jnp.swapaxes(update, 0, 1))


def solution(mesh):
    split = Mesh(mesh.devices.reshape(16, 4, 4, 2), ("z", "x", "y", "core"))
    spec = P(("y", "core"), ("z", "x"), None)
    return jax.shard_map(local, mesh=split, in_specs=(spec, spec), out_specs=(spec, spec), check_vma=False)
```

```python
import math

import jax
import jax.numpy as jnp
from jax import lax
from jax.experimental import pallas as pl
from jax.experimental.pallas import tpu as pltpu
from jax.sharding import Mesh, PartitionSpec as P

D = 1024
FF = 768
MATS = 8
HALF = D // 2
TILE = 384
BLOCKS = tuple(tuple(range(start, start + 8)) for start in range(0, 64, 8))
PLANES = ((0, 2, 4, 6, 9, 11, 13, 15), (1, 3, 5, 7, 8, 10, 12, 14))


MOMENTUM_RATE = 0.95
RMS_CAP = 0.5
NORM_EPS = 1e-07
COEF_A = 3.4445
COEF_B = -4.775
COEF_C = 2.0315


def dot_f32(left, right):
    return jnp.dot(left, right, preferred_element_type=jnp.float32)


def dot_transposed(left, right):
    return lax.dot_general(left, right, (((1,), (1,)), ((), ())), preferred_element_type=jnp.float32)


def call(kernel, out_shape, *args, scratch=(), cost=None, space=pltpu.VMEM, limit=32768):
    return pl.pallas_call(
        kernel,
        out_shape=out_shape,
        in_specs=[pl.BlockSpec(memory_space=space)] * len(args),
        out_specs=jax.tree.map(lambda _: pl.BlockSpec(memory_space=pltpu.VMEM), out_shape),
        scratch_shapes=scratch,
        compiler_params=pltpu.CompilerParams(vmem_limit_bytes=limit * 1024),
        cost_estimate=cost,
    )(*args)


def start_kernel(gradient, momentum, sums, kept, decayed, arrivals):
    copies = [
        pltpu.make_async_copy(gradient, kept, arrivals.at[0]),
        pltpu.make_async_copy(momentum, decayed, arrivals.at[1]),
    ]
    for copy in copies:
        copy.start()
    copies[0].wait()
    value = kept[...]
    sums[...] = jnp.broadcast_to(jnp.sum(value * value), sums.shape)
    copies[1].wait()
    decayed[...] = MOMENTUM_RATE * decayed[...]


def add_kernel(parts, out):
    out[...] = jnp.broadcast_to(jnp.sum(parts[...], axis=0, keepdims=True), out.shape)


def factor_of(total):
    total_square = jnp.sum(total[...], axis=0)[:, :1]
    factor = jnp.minimum(1.0, RMS_CAP * math.sqrt(MATS * MATS * FF * D) / jnp.sqrt(total_square))
    return factor[None]


def blend_kernel(total, gradient, decayed, outgoing):
    scaled = factor_of(total) * gradient[...]
    blended = jnp.swapaxes(scaled + MOMENTUM_RATE * (decayed[...] + scaled), 0, 1)
    left, right = blended[:, :, :HALF], blended[:, :, HALF:]
    packed = jnp.concatenate([left[:, :8], right[:, :8], left[:, 8:], right[:, 8:]], axis=1)
    outgoing[...] = packed.astype(jnp.bfloat16)


def copy_kernel(piece, out):
    value = piece[...].astype(jnp.float32)
    left, right = [], []
    for number in range(0, MATS, 2):
        first, second = value[number], value[number + 1]
        left += [first[:8], second[:8], first[16:20], second[16:20]]
        right += [first[8:16], second[8:16], first[20:], second[20:]]
    for start, parts in ((0, left), (HALF, right)):
        half = jnp.concatenate(parts, axis=0).astype(jnp.bfloat16)
        for number in range(MATS):
            out[number, :, start : start + HALF] = half


def packed_blocks(left, right):
    blocks = []
    for start in range(0, left.shape[0], 24):
        for place in range(2):
            head, tail = start + 8 * place, start + 16 + 4 * place
            blocks.append(
                jnp.concatenate(
                    [left[head : head + 8], right[head : head + 8], left[tail : tail + 4], right[tail : tail + 4]],
                    axis=0,
                )
            )
    return blocks


def orthogonal_kernel(whole, out, gram, poly, second):
    rows = FF // MATS
    tiles = [slice(start, start + TILE) for start in range(0, FF, TILE)]
    on_diagonal = lax.broadcasted_iota(jnp.int32, (TILE, TILE), 0) == lax.broadcasted_iota(
        jnp.int32, (TILE, TILE), 1
    )
    norm_square = jnp.float32(0.0)
    for tile in tiles:
        product = dot_transposed(whole[tile, :], whole[...])
        norm_square += jnp.sum(jnp.where(on_diagonal, product[:, tile], 0.0))
        gram[tile, :] = product.astype(jnp.bfloat16)
    inverse = 1.0 / (jnp.sqrt(jnp.full((1, 1), norm_square, jnp.float32)) + NORM_EPS)
    scale = inverse * inverse
    for tile in tiles:
        squared = scale * dot_f32(gram[tile, :], gram[...])
        poly[tile, :] = (
            scale * (COEF_B * gram[tile, :].astype(jnp.float32) + COEF_C * squared)
        ).astype(jnp.bfloat16)
    for tile in tiles:
        combined = COEF_A * whole[tile, :].astype(jnp.float32) + dot_f32(poly[tile, :], whole[...])
        second[tile, :] = (inverse * combined).astype(jnp.bfloat16)
    for tile in tiles:
        gram[tile, :] = dot_transposed(second[tile, :], second[...]).astype(jnp.bfloat16)
    member = lax.rem(lax.axis_index("z"), 2) * 4 + lax.axis_index("x")
    place = pl.ds(pl.multiple_of(member * rows, 32), rows)
    own = gram[place, :]
    own_poly = (COEF_B * own.astype(jnp.float32) + COEF_C * dot_f32(own, gram[...])).astype(
        jnp.bfloat16
    )
    combined = COEF_A * second[place, :].astype(jnp.float32) + dot_f32(own_poly, second[...])
    scaled = 0.2 * math.sqrt(max(FF, D)) * combined
    for number, block in enumerate(packed_blocks(scaled[:, :HALF], scaled[:, HALF:])):
        out[number] = block.astype(jnp.bfloat16)


def finish_kernel(total, gradient, decayed, arrived, momentum_next, out):
    momentum_next[...] = decayed[...] + factor_of(total) * gradient[...]
    value = arrived[...].astype(jnp.float32)
    left = jnp.concatenate([value[:, :8], value[:, 16:20]], axis=1)
    right = jnp.concatenate([value[:, 8:16], value[:, 20:]], axis=1)
    out[:, :, :HALF] = jnp.swapaxes(left, 0, 1).astype(jnp.bfloat16)
    out[:, :, HALF:] = jnp.swapaxes(right, 0, 1).astype(jnp.bfloat16)


def orthogonal_rows(whole):
    return call(
        orthogonal_kernel,
        jax.ShapeDtypeStruct((MATS, 24, HALF), jnp.bfloat16),
        whole,
        scratch=[
            pltpu.VMEM((FF, FF), jnp.bfloat16),
            pltpu.VMEM((FF, FF), jnp.bfloat16),
            pltpu.VMEM((FF, D), jnp.bfloat16),
        ],
        cost=pl.CostEstimate(
            flops=2 * FF * (3 * FF * D + FF * FF), bytes_accessed=2 * FF * D, transcendentals=0
        ),
    )


def exchanged(value, axes, groups=None):
    return lax.all_to_all(value, axes, split_axis=0, concat_axis=0, tiled=True, axis_index_groups=groups)


def gathered(piece):
    rows = FF // MATS
    copies = call(copy_kernel, jax.ShapeDtypeStruct((MATS, rows, D), piece.dtype), piece)
    return exchanged(copies, ("z", "x"), BLOCKS).reshape(FF, D)


def local(gradient, momentum):
    shape = (gradient.shape[1], MATS, D)
    gradient, momentum = jnp.swapaxes(gradient, 0, 1), jnp.swapaxes(momentum, 0, 1)
    whole = jax.ShapeDtypeStruct(shape, jnp.float32)
    squares, kept, decayed = call(
        start_kernel,
        (jax.ShapeDtypeStruct((32, 1, 128), jnp.float32), whole, whole),
        gradient,
        momentum,
        scratch=[pltpu.SemaphoreType.DMA((2,))],
        space=pl.ANY,
        limit=54272,
    )
    squares = exchanged(squares, ("x", "y", "core"))
    squares = call(add_kernel, jax.ShapeDtypeStruct((16, 1, 128), jnp.float32), squares)
    squares = exchanged(squares, "z")
    outgoing = call(
        blend_kernel, jax.ShapeDtypeStruct((MATS, 24, HALF), jnp.bfloat16), squares, kept, decayed
    )
    piece = exchanged(outgoing, "z", PLANES)
    returning = orthogonal_rows(gathered(piece))
    arrived = exchanged(returning, "z", PLANES)
    momentum_next, update = call(
        finish_kernel,
        (whole, jax.ShapeDtypeStruct(shape, jnp.bfloat16)),
        squares,
        kept,
        decayed,
        arrived,
    )
    return (jnp.swapaxes(momentum_next, 0, 1), jnp.swapaxes(update, 0, 1))


def solution(mesh):
    split = Mesh(mesh.devices.reshape(16, 4, 4, 2), ("z", "x", "y", "core"))
    spec = P(("y", "core"), ("z", "x"), None)
    return jax.shard_map(local, mesh=split, in_specs=(spec, spec), out_specs=(spec, spec), check_vma=False)
```
